256 devices in a mesh: row: 16 (over z, core), col: 16 (over x, y).
Axes of the slice: x: 4, y: 4, z: 8, core: 2. Of those that a mesh axis runs over, the one named last changes fastest.
Arguments:
- kernel: float32 [12288, 12288], P('row', 'col'), may hold values from 0 to 3.1, as said below
Outputs:
- factored: float32 [12288, 12288], P('row', 'col')
The draws below stay inside these ranges and needn't reach their ends.
Inputs may be any that keep to these rules, and one draw needn't show every extreme that they name: kernel is the block-cyclic storage of a symmetric positive definite matrix whose least eigenvalue is 0.5 or more.
All inputs are finite; a program needn't handle non-finite values.
Results may differ from the reference program's by a relative error of at most 0.0003.
Values sent between devices are 32-bit elements; how exact they have to be, the bound alone decides.
A program may use at most 64 MiB of HBM per device.

```python
import math
import jax
import jax.numpy as jnp
from jax import lax

NB = 256
SUBPANELS = 4
BLK_DEV = 3
BLK_COL = 3
ORDER = 12288
N_ROW = 16
N_COL = 16


feature_count = 1024


jitter_value = 0.5


def stored_index(count, per_dev, devs):
    stored = jnp.arange(count, dtype=jnp.int32)
    sblock = stored // NB
    gblock = sblock % per_dev * devs + sblock // per_dev
    return (gblock * NB + stored % NB).astype(jnp.int32)


def draw_kernel(key, part):
    first, second = jax.random.split(jax.random.fold_in(key, 7), 2)
    raw = jax.random.normal(first, (ORDER, feature_count), jnp.float32)
    radius = jnp.exp(jax.random.uniform(second, (ORDER,), jnp.float32, math.log(0.5), math.log(1.6)))
    length = jnp.sqrt(jnp.sum(raw * raw, axis=1))
    unit = raw / jnp.maximum(length, 0.1)[:, None]
    rows = stored_index(ORDER, BLK_DEV, N_ROW)
    cols = stored_index(ORDER, BLK_COL, N_COL)
    unit_rows = unit[rows]
    unit_cols = unit[cols]
    cosine = jnp.dot(unit_rows, unit_cols.T, precision=lax.Precision.HIGHEST, preferred_element_type=jnp.float32)
    cosine = jnp.clip(cosine, -1.0, 1.0)
    angle = jnp.arccos(cosine)
    shape_part = (jnp.sqrt(jnp.maximum(1.0 - cosine * cosine, 0.0)) + (math.pi - angle) * cosine) / math.pi
    radius_rows = radius[rows]
    radius_cols = radius[cols]
    scaled = radius_rows[:, None] * radius_cols[None, :] * shape_part
    same = rows[:, None] == cols[None, :]
    matrix = jnp.where(same, radius_rows[:, None] * radius_rows[:, None] + jitter_value, scaled)
    return matrix.astype(jnp.float32)


def setup_inputs(seed: int = 0) -> dict:
    arg_keys = jax.random.split(jax.random.key(seed), 2)
    return {
        "kernel": draw_kernel(jax.random.fold_in(arg_keys[1], 71), 0),
    }


def lower_inverse(factor):
    ident = jnp.eye(factor.shape[0], dtype=jnp.float32)
    return jax.scipy.linalg.solve_triangular(factor, ident, lower=True)

def stored_to_math(count, per_dev, devs):
    stored = jnp.arange(count, dtype=jnp.int32)
    sblock = stored // NB
    gblock = sblock % per_dev * devs + sblock // per_dev
    return (gblock * NB + stored % NB).astype(jnp.int32)

def math_to_stored(count, per_dev, devs):
    mrow = jnp.arange(count, dtype=jnp.int32)
    gblock = mrow // NB
    sblock = gblock % devs * per_dev + gblock // devs
    return (sblock * NB + mrow % NB).astype(jnp.int32)

def reference(kernel):
    row_src = math_to_stored(ORDER, BLK_DEV, N_ROW)
    col_src = math_to_stored(ORDER, BLK_COL, N_COL)
    matrix = kernel[row_src[:, None], col_src[None, :]]
    columns = []
    for sub_step in range(SUBPANELS):
        low = sub_step * NB
        high = low + NB
        factor = jnp.linalg.cholesky(matrix[low:high, low:high])
        inverse = lower_inverse(factor)
        below = jnp.dot(matrix[high:, low:high].astype(jnp.float32), inverse.T.astype(jnp.float32), precision=lax.Precision.HIGHEST, preferred_element_type=jnp.float32)
        update = jnp.dot(below.astype(jnp.float32), below.T.astype(jnp.float32), precision=lax.Precision.HIGHEST, preferred_element_type=jnp.float32)
        matrix = matrix.at[high:, high:].add(-update)
        columns.append(jnp.concatenate([jnp.zeros((low, NB), jnp.float32), factor, below], axis=0))
    for sub_step in range(SUBPANELS):
        matrix = matrix.at[:, sub_step * NB:(sub_step + 1) * NB].set(columns[sub_step])
    edge = SUBPANELS * NB
    matrix = matrix.at[:edge, edge:].set(jnp.zeros((edge, ORDER - edge), jnp.float32))
    row_back = stored_to_math(ORDER, BLK_DEV, N_ROW)
    col_back = stored_to_math(ORDER, BLK_COL, N_COL)
    return matrix[row_back[:, None], col_back[None, :]]
```

```python
import functools

import jax
import jax.numpy as jnp
from jax import lax
from jax.experimental import pallas as pl
from jax.experimental.pallas import tpu as pltpu
from jax.sharding import PartitionSpec as P

NB = 256
SUBPANELS = 4
MESH = pl.DeviceIdType.MESH
F32 = jnp.float32
BF16 = jnp.bfloat16


def split3(x):
    high = x.astype(BF16)
    rest = x - high.astype(F32)
    middle = rest.astype(BF16)
    low = (rest - middle.astype(F32)).astype(BF16)
    return high, middle, low


def split2(x):
    high = x.astype(BF16)
    return high, (x - high.astype(F32)).astype(BF16)


def dot_nn(a, b):
    return lax.dot_general(a, b, (((1,), (0,)), ((), ())), preferred_element_type=F32)


def dot_nt(a, b):
    return lax.dot_general(a, b, (((1,), (1,)), ((), ())), preferred_element_type=F32)


def dot3(dot, a, b):
    return dot(a[0], b[0]) + (dot(a[0], b[1]) + dot(a[1], b[0]))


def tree_sum(terms):
    while len(terms) > 1:
        terms = [sum(terms[i + 1 : i + 2], terms[i]) for i in range(0, len(terms), 2)]
    return terms[0]


def eliminate(tiles, s, first, active, iota):
    quarter, lane = divmod(first, 128)

    def spread(x):
        return jnp.broadcast_to(x, (8, 128))

    column = {
        t: [spread(tiles[t][quarter][:, lane + k : lane + k + 1]) for k in range(8)]
        for t in range(s, 4)
    }
    e = [[spread(column[s][k][i : i + 1, :]) if k <= i else None for k in range(8)] for i in range(8)]
    low = [[None] * 8 for _ in range(8)]
    inv = [[None] * 8 for _ in range(8)]
    for j in range(8):
        root = lax.rsqrt(e[j][j])
        for i in range(j + 1, 8):
            low[i][j] = e[i][j] * root
        for i in range(j + 1, 8):
            for k in range(j + 1, i + 1):
                e[i][k] = e[i][k] - low[i][j] * low[k][j]
        inv[j][j] = root
        for k in range(j):
            total = low[j][k] * inv[k][k]
            for m in range(k + 1, j):
                total = total + low[j][m] * inv[m][k]
            inv[j][k] = -(root * total)
    columns = []
    for k in range(8):
        value = inv[7][k]
        for i in range(6, k - 1, -1):
            value = jnp.where(iota == i, inv[i][k], value)
        if k > 0:
            value = jnp.where(iota < k, 0.0, value)
        columns.append(value)
    done = {
        q: tree_sum([columns[k] * spread(tiles[s][q][k : k + 1, :]) for k in range(8)])
        for q in active
    }
    for t in range(s + 1, 4):
        factor = [tree_sum([column[t][m] * inv[k][m] for m in range(k + 1)]) for k in range(8)]
        for q in active:
            tiles[t][q] = tiles[t][q] - tree_sum(
                [factor[k] * spread(done[q][k : k + 1, :]) for k in range(8)]
            )
    tiles[s].update(done)


def factor_block(work):
    iota = lax.broadcasted_iota(jnp.int32, (8, 128), 0)
    for slab in range(8):
        first = 32 * slab
        active = [0, 1, 2] if slab < 4 else [1, 2, 3]
        tiles = [
            {q: work[first + 8 * t : first + 8 * t + 8, 128 * q : 128 * q + 128] for q in active}
            for t in range(4)
        ]
        for s in range(4):
            eliminate(tiles, s, first + 8 * s, active, iota)
        for t in range(4):
            for q in active:
                work[first + 8 * t : first + 8 * t + 8, 128 * q : 128 * q + 128] = tiles[t][q]
        if slab == 7:
            break
        left = 128 * active[0]
        top = jnp.concatenate(
            [jnp.concatenate([tiles[t][q] for q in active], axis=1) for t in range(4)], axis=0
        )
        high, middle, low = split3(top)
        right = jnp.concatenate([high, middle, high, middle, low, high], axis=0)
        across = top[:, : 256 - left].T
        high, middle, low = split3(across)
        down = jnp.concatenate([high, high, middle, middle, high, low], axis=1)
        for begin, end in ((first + 32, first + 64), (first + 64, 256)):
            if begin < end:
                work[begin:end, left : left + 384] = work[begin:end, left : left + 384] - dot_nn(
                    down[begin - left : end - left], right
                )


def solve_kernel(
    a_ref, corner_ref, rows_ref, cols_ref, o_ref,
    work, corner, inv2, low2, p2, v2, total,
):
    row, col = lax.axis_index("row"), lax.axis_index("col")
    iota_r = lax.broadcasted_iota(jnp.int32, (NB, NB), 0)
    iota_c = lax.broadcasted_iota(jnp.int32, (NB, NB), 1)
    eye = jnp.where(iota_r == iota_c, 1.0, 0.0).astype(F32)
    corner[...] = corner_ref[...]
    total[...] = a_ref[...]

    def store2(ref, index, value):
        high, low = split2(value)
        ref[index, 0] = high
        ref[index, 1] = low

    def load2(ref, index):
        return ref[index, 0], ref[index, 1]

    def step(k, _):
        work[:, 0:NB] = corner[k, k]
        work[:, NB : 2 * NB] = eye
        factor_block(work)
        inverse = jnp.where(iota_r >= iota_c, work[:, NB : 2 * NB], 0.0)
        store2(inv2, 0, inverse)
        inv = load2(inv2, 0)

        def below(i, _):
            store2(low2, i * SUBPANELS + k, dot3(dot_nt, split2(corner[i, k]), inv))
            return 0

        lax.fori_loop(k + 1, SUBPANELS, below, 0)

        def trail(i, _):
            def inner(j, _):
                corner[i, j] = corner[i, j] - dot3(
                    dot_nt, load2(low2, i * SUBPANELS + k), load2(low2, j * SUBPANELS + k)
                )
                return 0

            return lax.fori_loop(k + 1, i + 1, inner, 0)

        lax.fori_loop(k + 1, SUBPANELS, trail, 0)

        def rest(m, carry):
            across, down = carry
            low = load2(low2, k * SUBPANELS + m)
            return (
                across - dot3(dot_nt, load2(p2, m), low),
                down - dot3(dot_nn, low, load2(v2, m)),
            )

        across, down = lax.fori_loop(0, k, rest, (rows_ref[k], cols_ref[k]))
        p = dot3(dot_nt, split2(across), inv)
        store2(p2, k, p)
        store2(v2, k, dot3(dot_nn, inv, split2(down)))
        total[...] = total[...] - dot3(dot_nn, load2(p2, k), load2(v2, k))

        @pl.when(col == k)
        def _():
            o_ref[:, 0:NB] = p

        return 0

    lax.fori_loop(0, SUBPANELS, step, 0)
    top = row < SUBPANELS
    left = col < SUBPANELS
    o_ref[:, NB:] = total[:, NB:]

    @pl.when(jnp.logical_not(left))
    def _():
        o_ref[:, 0:NB] = total[:, 0:NB]

    @pl.when(top)
    def _():
        o_ref[0:NB, NB:] = jnp.zeros((NB, 2 * NB), F32)

    @pl.when(jnp.logical_and(top, col > row))
    def _():
        o_ref[0:NB, 0:NB] = jnp.zeros((NB, NB), F32)

    @pl.when(jnp.logical_and(top, col == row))
    def _():
        o_ref[0:NB, 0:NB] = jnp.where(iota_r >= iota_c, o_ref[0:NB, 0:NB], 0.0)


def solve(a, corner, rows, cols):
    size = a.shape[0]
    vmem = pl.BlockSpec(memory_space=pltpu.VMEM)
    return pl.pallas_call(
        solve_kernel,
        out_shape=jax.ShapeDtypeStruct(a.shape, F32),
        in_specs=[vmem] * 4,
        out_specs=vmem,
        scratch_shapes=[
            pltpu.VMEM((NB, 2 * NB), F32),
            pltpu.VMEM((SUBPANELS, SUBPANELS, NB, NB), F32),
            pltpu.VMEM((1, 2, NB, NB), BF16),
            pltpu.VMEM((SUBPANELS * SUBPANELS, 2, NB, NB), BF16),
            pltpu.VMEM((SUBPANELS, 2, size, NB), BF16),
            pltpu.VMEM((SUBPANELS, 2, NB, size), BF16),
            pltpu.VMEM(a.shape, F32),
        ],
        compiler_params=pltpu.CompilerParams(vmem_limit_bytes=52 << 20),
        name="factor_and_update",
    )(a, corner, rows, cols)


def gather_kernel(
    a_ref, corner, rows, cols,
    z_send, z_recv, pair_send, pair_recv, x_send, x_recv, x_next, y_send, y_recv, y_next,
    d_send, d_recv, local,
):
    row, col = lax.axis_index("row"), lax.axis_index("col")
    z, core = row // 2, row % 2
    x, y = col // 4, col % 4

    def at(zz, cc, xx, yy):
        return (zz * 2 + cc, xx * 4 + yy)

    def remote(src, dst, send, recv, where):
        return pltpu.make_async_remote_copy(
            src_ref=src, dst_ref=dst, send_sem=send, recv_sem=recv,
            device_id=where, device_id_type=MESH,
        )

    up, down = at((z + 1) % 8, core, x, y), at((z + 7) % 8, core, x, y)
    pair = at(z, 1 - core, x, y)
    east, west = at(z, core, (x + 1) % 4, y), at(z, core, (x + 3) % 4, y)
    north, south = at(z, core, x, (y + 1) % 4), at(z, core, x, (y + 3) % 4)

    barrier = pltpu.get_barrier_semaphore()
    peers = (up, down, pair, east, west, north, south)
    for peer in peers:
        pl.semaphore_signal(barrier, inc=1, device_id=peer, device_id_type=MESH)
    pl.semaphore_wait(barrier, len(peers))

    @pl.when(row < SUBPANELS)
    def _():
        copy = pltpu.make_async_copy(a_ref.at[0:NB, :], cols.at[row], local.at[0])
        copy.start()
        copy.wait()

    @pl.when(x == 0)
    def _():
        copy = pltpu.make_async_copy(a_ref.at[:, 0:NB], rows.at[y], local.at[1])
        copy.start()
        copy.wait()

    def col_piece(slab, block):
        return cols.at[slab, :, block * NB : (block + 1) * NB]

    def z_copy(item, where, direction):
        half, block = item % 2, item // 2
        piece = col_piece(2 * half + core, block)
        return remote(piece, piece, z_send.at[item, direction], z_recv.at[item], where)

    def pair_copy(item, which):
        half, block = item % 2, item // 2
        piece = col_piece(2 * half + which, block)
        return remote(piece, piece, pair_send.at[item], pair_recv.at[item], pair)

    def z_route(half):
        if half == 0:
            return z <= 3, jnp.logical_or(z == 0, z >= 6)
        return jnp.logical_and(z >= 1, z <= 3), jnp.logical_or(z <= 1, z >= 6)

    def z_step(item):
        half = item % 2
        own = z == half

        @pl.when(jnp.logical_not(own))
        def _():
            z_copy(item, up, 0).wait_recv()

        to_up, to_down = z_route(half)

        @pl.when(to_up)
        def _():
            z_copy(item, up, 0).start()

        @pl.when(to_down)
        def _():
            z_copy(item, down, 1).start()

        pair_copy(item, core).start()

    def z_finish(item):
        half = item % 2
        to_up, to_down = z_route(half)

        @pl.when(to_up)
        def _():
            z_copy(item, up, 0).wait_send()

        @pl.when(to_down)
        def _():
            z_copy(item, down, 1).wait_send()

        pair_copy(item, core).wait_send()
        pair_copy(item, 1 - core).wait_recv()

    def item_ref(item, source, part):
        if item < 2:
            ref = corner.at[2 * item + core, source]
            base = 0
        else:
            ref = rows.at[source]
            base = (item - 2) * NB
        if part is None:
            return ref.at[base : base + NB, :]
        return ref.at[base + part * 128 : base + part * 128 + 128, :]

    def wanted(item, source):
        if item >= 2:
            return source >= 0
        return 2 * item + core >= source

    def whole(item, where, slot, recv):
        ref = item_ref(item, y, None)
        return remote(ref, ref, x_send.at[item, slot], recv, where)

    def x_half(item, part, where):
        ref = item_ref(item, y, part)
        return remote(ref, ref, x_send.at[item, 0], x_next.at[item, part], where)

    def x_step(item):
        ok = wanted(item, y)
        if item < 2:
            @pl.when(x == 0)
            def _():
                copy = pltpu.make_async_copy(
                    cols.at[2 * item + core, :, 0:NB], corner.at[2 * item + core, y], local.at[0]
                )
                copy.start()
                copy.wait()

        @pl.when(jnp.logical_and(ok, x == 0))
        def _():
            whole(item, east, 0, x_recv.at[item]).start()
            whole(item, west, 1, x_recv.at[item]).start()

        @pl.when(jnp.logical_and(ok, x == 1))
        def _():
            whole(item, east, 0, x_recv.at[item]).wait_recv()
            x_half(item, 0, east).start()

        @pl.when(jnp.logical_and(ok, x == 3))
        def _():
            whole(item, east, 0, x_recv.at[item]).wait_recv()
            x_half(item, 1, west).start()

        @pl.when(jnp.logical_and(ok, x == 2))
        def _():
            x_half(item, 0, east).wait_recv()
            x_half(item, 1, east).wait_recv()

    def x_finish(item):
        ok = wanted(item, y)

        @pl.when(jnp.logical_and(ok, x == 0))
        def _():
            whole(item, east, 0, x_recv.at[item]).wait_send()
            whole(item, west, 1, x_recv.at[item]).wait_send()

        @pl.when(jnp.logical_and(ok, x == 1))
        def _():
            x_half(item, 0, east).wait_send()

        @pl.when(jnp.logical_and(ok, x == 3))
        def _():
            x_half(item, 1, west).wait_send()

    def y_whole(item, source, side):
        ref = item_ref(item, source, None)
        return remote(
            ref, ref, y_send.at[item, side], y_recv.at[item, side], north if side == 0 else south
        )

    def y_half(item, source, side):
        ref = item_ref(item, source, side)
        return remote(
            ref, ref, y_send.at[item, 2 + side], y_next.at[item, side], north if side == 0 else south
        )

    before, after, opposite = (y + 3) % 4, (y + 1) % 4, (y + 2) % 4

    def y_start(item):
        @pl.when(wanted(item, y))
        def _():
            y_whole(item, y, 0).start()
            y_whole(item, y, 1).start()

    def y_step(item):
        @pl.when(wanted(item, before))
        def _():
            y_whole(item, before, 0).wait_recv()
            y_half(item, before, 0).start()

        @pl.when(wanted(item, after))
        def _():
            y_whole(item, after, 1).wait_recv()
            y_half(item, after, 1).start()

    def y_finish(item):
        @pl.when(wanted(item, opposite))
        def _():
            y_half(item, opposite, 0).wait_recv()
            y_half(item, opposite, 1).wait_recv()

        @pl.when(wanted(item, y))
        def _():
            y_whole(item, y, 0).wait_send()
            y_whole(item, y, 1).wait_send()

        @pl.when(wanted(item, before))
        def _():
            y_half(item, before, 0).wait_send()

        @pl.when(wanted(item, after))
        def _():
            y_half(item, after, 1).wait_send()

    def corner_copy(item, source, which):
        ref = corner.at[2 * item + which, source]
        return remote(ref, ref, d_send.at[item, source], d_recv.at[item, source], pair)

    def corner_each(item, which, action):
        for source in range(4):
            @pl.when(2 * item + which >= source)
            def _():
                action(corner_copy(item, source, which))

    def corner_start(item):
        corner_each(item, core, lambda c: c.start())

    def corner_finish(item):
        corner_each(item, core, lambda c: c.wait_send())
        corner_each(item, 1 - core, lambda c: c.wait_recv())

    order = (0, 1, 2, 3, 4)
    z_step(0)
    z_step(1)
    for item in order:
        x_step(item)
        y_start(item)
        if item >= 1:
            y_step(item - 1)
            z_step(item + 1)
    y_step(4)
    for item in order:
        x_finish(item)
        y_finish(item)
        if item < 2:
            corner_start(item)
    for item in range(2):
        corner_finish(item)
    for item in range(6):
        z_finish(item)


def gather(a):
    size = a.shape[0]
    hbm = pl.BlockSpec(memory_space=pl.ANY)
    dma = pltpu.SemaphoreType.DMA
    return pl.pallas_call(
        gather_kernel,
        out_shape=[
            jax.ShapeDtypeStruct((SUBPANELS, SUBPANELS, NB, NB), F32),
            jax.ShapeDtypeStruct((SUBPANELS, size, NB), F32),
            jax.ShapeDtypeStruct((SUBPANELS, NB, size), F32),
        ],
        in_specs=[hbm],
        out_specs=[hbm] * 3,
        scratch_shapes=[
            dma((6, 2)), dma((6,)), dma((6,)), dma((6,)),
            dma((5, 2)), dma((5,)), dma((5, 2)),
            dma((5, 4)), dma((5, 2)), dma((5, 2)),
            dma((2, 4)), dma((2, 4)), dma((2,)),
        ],
        compiler_params=pltpu.CompilerParams(collective_id=0, has_side_effects=True),
        name="gather_panels",
    )(a)


def body(kernel):
    corner, rows, cols = gather(kernel)
    return solve(kernel, corner, rows, cols)


def solution(mesh):
    return jax.shard_map(
        body,
        mesh=mesh,
        in_specs=(P("row", "col"),),
        out_specs=P("row", "col"),
        check_vma=False,
    )
```

```python
import functools

import jax
import jax.numpy as jnp
from jax import lax
from jax.experimental import pallas as pl
from jax.experimental.pallas import tpu as pltpu
from jax.sharding import PartitionSpec as P

NB = 256
SUBPANELS = 4
MESH = pl.DeviceIdType.MESH
F32 = jnp.float32
BF16 = jnp.bfloat16


def split3(x):
    high = x.astype(BF16)
    rest = x - high.astype(F32)
    middle = rest.astype(BF16)
    low = (rest - middle.astype(F32)).astype(BF16)
    return high, middle, low


def split2(x):
    high = x.astype(BF16)
    return high, (x - high.astype(F32)).astype(BF16)


def dot_nn(a, b):
    return lax.dot_general(a, b, (((1,), (0,)), ((), ())), preferred_element_type=F32)


def dot_nt(a, b):
    return lax.dot_general(a, b, (((1,), (1,)), ((), ())), preferred_element_type=F32)


def dot3(dot, a, b):
    return dot(a[0], b[0]) + (dot(a[0], b[1]) + dot(a[1], b[0]))


def tree_sum(terms):
    while len(terms) > 1:
        terms = [sum(terms[i + 1 : i + 2], terms[i]) for i in range(0, len(terms), 2)]
    return terms[0]


def eliminate(tiles, s, first, active, iota):
    quarter, lane = divmod(first, 128)

    def spread(x):
        return jnp.broadcast_to(x, (8, 128))

    column = {
        t: [spread(tiles[t][quarter][:, lane + k : lane + k + 1]) for k in range(8)]
        for t in range(s, 4)
    }
    e = [[spread(column[s][k][i : i + 1, :]) if k <= i else None for k in range(8)] for i in range(8)]
    low = [[None] * 8 for _ in range(8)]
    inv = [[None] * 8 for _ in range(8)]
    for j in range(8):
        root = lax.rsqrt(e[j][j])
        for i in range(j + 1, 8):
            low[i][j] = e[i][j] * root
        for i in range(j + 1, 8):
            for k in range(j + 1, i + 1):
                e[i][k] = e[i][k] - low[i][j] * low[k][j]
        inv[j][j] = root
        for k in range(j):
            total = low[j][k] * inv[k][k]
            for m in range(k + 1, j):
                total = total + low[j][m] * inv[m][k]
            inv[j][k] = -(root * total)
    columns = []
    for k in range(8):
        value = inv[7][k]
        for i in range(6, k - 1, -1):
            value = jnp.where(iota == i, inv[i][k], value)
        if k > 0:
            value = jnp.where(iota < k, 0.0, value)
        columns.append(value)
    done = {
        q: tree_sum([columns[k] * spread(tiles[s][q][k : k + 1, :]) for k in range(8)])
        for q in active
    }
    for t in range(s + 1, 4):
        factor = [tree_sum([column[t][m] * inv[k][m] for m in range(k + 1)]) for k in range(8)]
        for q in active:
            tiles[t][q] = tiles[t][q] - tree_sum(
                [factor[k] * spread(done[q][k : k + 1, :]) for k in range(8)]
            )
    tiles[s].update(done)


def factor_block(work):
    iota = lax.broadcasted_iota(jnp.int32, (8, 128), 0)
    for slab in range(8):
        first = 32 * slab
        active = [0, 1, 2] if slab < 4 else [1, 2, 3]
        tiles = [
            {q: work[first + 8 * t : first + 8 * t + 8, 128 * q : 128 * q + 128] for q in active}
            for t in range(4)
        ]
        for s in range(4):
            eliminate(tiles, s, first + 8 * s, active, iota)
        for t in range(4):
            for q in active:
                work[first + 8 * t : first + 8 * t + 8, 128 * q : 128 * q + 128] = tiles[t][q]
        if slab == 7:
            break
        left = 128 * active[0]
        top = jnp.concatenate(
            [jnp.concatenate([tiles[t][q] for q in active], axis=1) for t in range(4)], axis=0
        )
        high, middle, low = split3(top)
        right = jnp.concatenate([high, middle, high, middle, low, high], axis=0)
        across = top[:, : 256 - left].T
        high, middle, low = split3(across)
        down = jnp.concatenate([high, high, middle, middle, high, low], axis=1)
        for begin, end in ((first + 32, first + 64), (first + 64, 256)):
            if begin < end:
                work[begin:end, left : left + 384] = work[begin:end, left : left + 384] - dot_nn(
                    down[begin - left : end - left], right
                )


ROW_CHUNKS = 6
RING_CHUNKS = 8
RING_LAG = 3
RING_STEPS = RING_CHUNKS + 5 * RING_LAG + 1


def factor_kernel(
    a_ref, o_ref,
    rows, cols, low, corner, work, p2, v2, column,
    local, c_send, c_recv, x_send, x_recv, y_send, y_recv, z_send, z_extra, z_recv,
    q_send, q_recv, r_send, r_recv, s_send, s_recv, t_send, t_recv,
    u_send, u_recv, w_send, w_recv, e_send, e_recv,
):
    size = a_ref.shape[0]
    row, col = lax.axis_index("row"), lax.axis_index("col")
    z, core = row // 2, row % 2
    x, y = col // 4, col % 4
    both, either, no = jnp.logical_and, jnp.logical_or, jnp.logical_not
    is_root = both(row == 0, col == 0)
    is_spreader = both(row == 1, col == 0)
    root, spreader = (0, 0), (1, 0)

    def at(zz, cc, xx, yy):
        return (zz * 2 + cc, xx * 4 + yy)

    def ring(step):
        return at((z + step) % 8, core, x, y)

    def plane(dx, dy):
        return at(z, core, (x + dx) % 4, (y + dy) % 4)

    pair = at(z, 1 - core, x, y)

    def remote(ref, send, recv, where, src=None):
        return pltpu.make_async_remote_copy(
            src_ref=ref if src is None else src, dst_ref=ref, send_sem=send, recv_sem=recv,
            device_id=where, device_id_type=MESH,
        )

    barrier = pltpu.get_barrier_semaphore()
    offsets = [(dx, dy) for dx in range(4) for dy in range(4) if dx or dy]
    peers = [ring(step) for step in range(1, 8)] + [plane(*o) for o in offsets] + [pair]
    for peer in peers:
        pl.semaphore_signal(barrier, inc=1, device_id=peer, device_id_type=MESH)
    owners = [(i, j) for i in range(SUBPANELS) for j in range(i + 1) if i or j]
    owner = both(both(row < SUBPANELS, col <= row), no(is_root))

    @pl.when(owner)
    def _():
        pl.semaphore_signal(barrier, inc=1, device_id=root, device_id_type=MESH)

    @pl.when(is_root)
    def _():
        for peer in owners:
            pl.semaphore_signal(barrier, inc=1, device_id=peer, device_id_type=MESH)

    keep = pltpu.make_async_copy(a_ref, o_ref, local.at[0])
    keep.start()
    own_cols = pltpu.make_async_copy(a_ref.at[0:NB, :], cols.at[row % SUBPANELS], local.at[1])
    own_rows = pltpu.make_async_copy(a_ref.at[:, 0:NB], rows.at[y], local.at[2])
    own_corner = pltpu.make_async_copy(a_ref.at[0:NB, 0:NB], corner.at[0, 0], local.at[3])
    pl.when(row < SUBPANELS)(own_cols.start)
    pl.when(x == 0)(own_rows.start)
    pl.when(is_root)(own_corner.start)
    total = len(peers) + jnp.where(owner, 1, 0) + jnp.where(is_root, len(owners), 0)
    pl.semaphore_wait(barrier, total)

    def corner_copy(i, j):
        return remote(
            corner.at[i, j], c_send.at[0], c_recv.at[i * SUBPANELS + j], root,
            src=a_ref.at[0:NB, 0:NB],
        )

    for i, j in owners:
        pl.when(both(row == i, col == j))(corner_copy(i, j).start)
    pl.when(row < SUBPANELS)(own_cols.wait)
    pl.when(x == 0)(own_rows.wait)

    def row_ref(source, chunk):
        length = size // ROW_CHUNKS
        return rows.at[source, chunk * length : (chunk + 1) * length, :]

    def x_copy(chunk, d):
        return remote(row_ref(y, chunk), x_send.at[chunk, d - 1], x_recv.at[chunk], plane(d, 0))

    def y_copy(chunk, d):
        return remote(
            row_ref(y, chunk), y_send.at[chunk, d - 1], y_recv.at[chunk, d - 1], plane(0, d)
        )

    def y_arrival(chunk, d):
        return remote(
            row_ref((y + 4 - d) % 4, chunk), y_send.at[chunk, d - 1], y_recv.at[chunk, d - 1], pair
        )

    def ring_ref(u, way, chunk):
        length = NB // 2 // RING_CHUNKS
        begin = pl.multiple_of(way * (NB // 2) + chunk * length, length)
        return cols.at[2 * u + core, pl.ds(begin, length), :]

    def distance(u, way):
        return (z - u + 8) % 8 if way == 0 else (u - z + 8) % 8

    def ring_copy(u, way, chunk):
        step = 1 if way == 0 else 7
        if (u, way) == (1, 1):
            where = at(jnp.where(z == 1, 7, (z + 7) % 8), core, x, y)
        else:
            where = ring(step)
        return remote(
            ring_ref(u, way, chunk), z_send.at[u, way, chunk], z_recv.at[u, way, chunk], where
        )

    def ring_second(chunk):
        return remote(ring_ref(1, 1, chunk), z_extra.at[chunk], z_recv.at[1, 1, chunk], ring(7))

    def ring_passes(u, way):
        passes = distance(u, way) < 7
        return both(passes, z != 0) if (u, way) == (1, 1) else passes

    def each_chunk(action):
        def one(chunk, _):
            action(chunk)
            return 0

        lax.fori_loop(0, RING_CHUNKS, one, 0)

    def slab_copy(u, which):
        return remote(cols.at[2 * u + which], q_send.at[u], q_recv.at[u], pair)

    @pl.when(x == 0)
    def _():
        for chunk in range(ROW_CHUNKS):
            for d in range(1, 4):
                x_copy(chunk, d).start()
                y_copy(chunk, d).start()

    def ring_start(chunk):
        for u in range(2):
            @pl.when(z == u)
            def _():
                for way in range(2):
                    ring_copy(u, way, chunk).start()
                if u == 1:
                    ring_second(chunk).start()

    each_chunk(ring_start)

    def group(k, begin, length):
        return low.at[k, 0 : SUBPANELS - k, pl.ds(begin, length), :]

    def give(k):
        return remote(group(k, 0, NB), r_send.at[k], r_recv.at[k], spreader)

    def deal(k, dx, dy):
        piece = (4 * dy + dx) * 16
        return remote(
            group(k, piece, 16), s_send.at[k, 4 * dx + dy - 1], s_recv.at[k], (1, dx * 4 + dy)
        )

    mine = pl.multiple_of((4 * y + x) * 16, 16)

    def climb(k, step):
        return remote(group(k, mine, 16), t_send.at[k, step - 1], t_recv.at[k], ring(step))

    def spread_x(k, d):
        return remote(group(k, mine, 16), u_send.at[k, d - 1], u_recv.at[k, d - 1], plane(d, 0))

    def spread_x_arrival(k, d):
        begin = pl.multiple_of((4 * y + (x + 4 - d) % 4) * 16, 16)
        return remote(group(k, begin, 16), u_send.at[k, d - 1], u_recv.at[k, d - 1], pair)

    def spread_y(k, d):
        begin = pl.multiple_of(y * 64, 64)
        return remote(group(k, begin, 64), w_send.at[k, d - 1], w_recv.at[k, d - 1], plane(0, d))

    def spread_y_arrival(k, d):
        begin = pl.multiple_of((y + 4 - d) % 4 * 64, 64)
        return remote(group(k, begin, 64), w_send.at[k, d - 1], w_recv.at[k, d - 1], pair)

    def to_pair(k):
        return remote(group(k, 0, NB), e_send.at[k], e_recv.at[k], pair)

    def x_goes(d):
        return both(core == 1, no(both(both(z == 0, y == 0), (x + d) % 4 == 0)))

    def y_goes(d):
        return both(core == 1, no(both(both(z == 0, x == 0), (y + d) % 4 == 0)))

    takes = both(core == 1, no(is_spreader))

    def stage1(k):
        @pl.when(is_spreader)
        def _():
            give(k).wait_recv()
            for dx, dy in offsets:
                deal(k, dx, dy).start()

    def stage2(k):
        @pl.when(both(core == 1, z == 0))
        def _():
            @pl.when(no(is_spreader))
            def _():
                remote(group(k, mine, 16), r_send.at[k], s_recv.at[k], pair).wait_recv()

            for step in range(1, 8):
                climb(k, step).start()

    def stage3(k):
        @pl.when(both(core == 1, z != 0))
        def _():
            climb(k, 1).wait_recv()

        for d in range(1, 4):
            pl.when(x_goes(d))(spread_x(k, d).start)

    def stage4(k):
        @pl.when(takes)
        def _():
            for d in range(1, 4):
                spread_x_arrival(k, d).wait_recv()

        for d in range(1, 4):
            pl.when(y_goes(d))(spread_y(k, d).start)

    def stage5(k):
        @pl.when(takes)
        def _():
            for d in range(1, 4):
                spread_y_arrival(k, d).wait_recv()
            to_pair(k).start()

        @pl.when(both(core == 0, no(is_root)))
        def _():
            to_pair(k).wait_recv()

    def group_sent(k):
        pl.when(is_root)(give(k).wait_send)

        @pl.when(is_spreader)
        def _():
            for dx, dy in offsets:
                deal(k, dx, dy).wait_send()

        @pl.when(both(core == 1, z == 0))
        def _():
            for step in range(1, 8):
                climb(k, step).wait_send()

        for d in range(1, 4):
            pl.when(x_goes(d))(spread_x(k, d).wait_send)
            pl.when(y_goes(d))(spread_y(k, d).wait_send)
        pl.when(takes)(to_pair(k).wait_send)

    iota_r = lax.broadcasted_iota(jnp.int32, (NB, NB), 0)
    iota_c = lax.broadcasted_iota(jnp.int32, (NB, NB), 1)

    def ring_step(n):
        for u in range(2):
            for way in range(2):
                away = distance(u, way)
                chunk = n - RING_LAG * (away - 1)

                @pl.when(
                    both(both(away > 0, ring_passes(u, way)), both(chunk >= 0, chunk < RING_CHUNKS))
                )
                def _():
                    copy = ring_copy(u, way, chunk)
                    copy.wait_recv()
                    copy.start()

    def row_step(chunk):
        @pl.when(x != 0)
        def _():
            x_copy(chunk, 1).wait_recv()
            for d in range(1, 4):
                y_copy(chunk, d).start()

    def ring_finish():
        for u in range(2):
            for way in range(2):
                @pl.when(both(distance(u, way) > 0, no(ring_passes(u, way))))
                def _():
                    each_chunk(lambda chunk: ring_copy(u, way, chunk).wait_recv())

            slab_copy(u, core).start()

    def slabs_arrived():
        for chunk in range(ROW_CHUNKS):
            for d in range(1, 4):
                y_arrival(chunk, d).wait_recv()
        for u in range(2):
            slab_copy(u, 1 - core).wait_recv()
        keep.wait()

    def store2(ref, index, value):
        high, rest = split2(value)
        ref[index, 0] = high
        ref[index, 1] = rest

    def load2(ref, index):
        return ref[index, 0], ref[index, 1]

    def update(k):
        inv = split2(low[k, 0])
        across, down = rows[k], cols[k]

        def rest(m, carry):
            across, down = carry
            block = split2(low[m, k - m])
            return (
                across - dot3(dot_nt, load2(p2, m), block),
                down - dot3(dot_nn, block, load2(v2, m)),
            )

        across, down = lax.fori_loop(0, k, rest, (across, down))
        p = dot3(dot_nt, split2(across), inv)
        store2(p2, k, p)
        store2(v2, k, dot3(dot_nn, inv, split2(down)))
        o_ref[...] = o_ref[...] - dot3(dot_nn, load2(p2, k), load2(v2, k))

        @pl.when(col == k)
        def _():
            column[...] = p

    @pl.when(is_root)
    def _():
        own_corner.wait()
        eye = jnp.where(iota_r == iota_c, 1.0, 0.0).astype(F32)

        def step(k, _):
            work[:, 0:NB] = corner[k, k]
            work[:, NB : 2 * NB] = eye
            factor_block(work)
            inverse = jnp.where(iota_r >= iota_c, work[:, NB : 2 * NB], 0.0)
            low[k, 0] = inverse
            inv = split2(inverse)

            @pl.when(k == 0)
            def _():
                for i, j in owners:
                    corner_copy(i, j).wait_recv()

            def below(i, _):
                low[k, i - k] = dot3(dot_nt, split2(corner[i, k]), inv)
                return 0

            lax.fori_loop(k + 1, SUBPANELS, below, 0)
            for fixed in range(SUBPANELS):
                pl.when(k == fixed)(give(fixed).start)

            def trail(i, _):
                def inner(j, _):
                    corner[i, j] = corner[i, j] - dot3(
                        dot_nt, split2(low[k, i - k]), split2(low[k, j - k])
                    )
                    return 0

                return lax.fori_loop(k + 1, i + 1, inner, 0)

            return lax.fori_loop(k + 1, SUBPANELS, trail, 0)

        lax.fori_loop(0, SUBPANELS, step, 0)
        ring_finish()
        slabs_arrived()
        lax.fori_loop(0, SUBPANELS, lambda k, c: (update(k), c)[1], 0)

    @pl.when(no(is_root))
    def _():
        plan = {
            8: [(stage1, 0)], 13: [(stage2, 0)], 17: [(stage3, 0)], 18: [(stage1, 1)],
            20: [(stage4, 0)], 22: [(stage2, 1)], 23: [(stage5, 0)],
        }
        for chunk in range(ROW_CHUNKS):
            plan.setdefault(3 + 4 * chunk, []).append((row_step, chunk))

        def one(n, _):
            ring_step(n)
            for when, actions in plan.items():
                @pl.when(n == when)
                def _():
                    for action, argument in actions:
                        action(argument)

            return 0

        lax.fori_loop(0, RING_STEPS, one, 0)
        stage3(1)
        ring_finish()
        stage1(2)
        stage4(1)
        stage2(2)
        stage5(1)

        def duties():
            stage3(2)
            stage1(3)
            stage4(2)
            stage2(3)

        pl.when(is_spreader)(duties)
        slabs_arrived()

        def some(k, _):
            update(k)
            for fixed in range(SUBPANELS - 1):
                @pl.when(k == fixed)
                def _():
                    if fixed == 0:
                        pl.when(no(is_spreader))(duties)
                    if fixed == 1:
                        stage5(2)
                    if fixed == 2:
                        stage3(3)
                        stage4(3)
                        stage5(3)

            return 0

        lax.fori_loop(0, SUBPANELS, some, 0)

    top, left = row < SUBPANELS, col < SUBPANELS

    @pl.when(left)
    def _():
        o_ref[:, 0:NB] = column[...]

    @pl.when(top)
    def _():
        o_ref[0:NB, NB:] = jnp.zeros((NB, size - NB), F32)

    @pl.when(both(top, col > row))
    def _():
        o_ref[0:NB, 0:NB] = jnp.zeros((NB, NB), F32)

    @pl.when(both(top, col == row))
    def _():
        o_ref[0:NB, 0:NB] = jnp.where(iota_r >= iota_c, o_ref[0:NB, 0:NB], 0.0)

    pl.when(owner)(corner_copy(0, 0).wait_send)

    @pl.when(x == 0)
    def _():
        for chunk in range(ROW_CHUNKS):
            for d in range(1, 4):
                x_copy(chunk, d).wait_send()

    for chunk in range(ROW_CHUNKS):
        for d in range(1, 4):
            y_copy(chunk, d).wait_send()
    for u in range(2):
        for way in range(2):
            @pl.when(ring_passes(u, way))
            def _():
                each_chunk(lambda chunk: ring_copy(u, way, chunk).wait_send())

        slab_copy(u, core).wait_send()
    pl.when(z == 1)(lambda: each_chunk(lambda chunk: ring_second(chunk).wait_send()))
    for k in range(SUBPANELS):
        group_sent(k)


def body(a):
    size = a.shape[0]
    dma = pltpu.SemaphoreType.DMA
    vmem = pltpu.VMEM
    return pl.pallas_call(
        factor_kernel,
        out_shape=jax.ShapeDtypeStruct(a.shape, F32),
        in_specs=[pl.BlockSpec(memory_space=pl.ANY)],
        out_specs=pl.BlockSpec(memory_space=pltpu.VMEM),
        scratch_shapes=[
            vmem((SUBPANELS, size, NB), F32),
            vmem((SUBPANELS, NB, size), F32),
            vmem((SUBPANELS, SUBPANELS, NB, NB), F32),
            vmem((SUBPANELS, SUBPANELS, NB, NB), F32),
            vmem((NB, 2 * NB), F32),
            vmem((SUBPANELS, 2, size, NB), BF16),
            vmem((SUBPANELS, 2, NB, size), BF16),
            vmem((size, NB), F32),
            dma((4,)),
            dma((1,)), dma((16,)),
            dma((ROW_CHUNKS, 3)), dma((ROW_CHUNKS,)),
            dma((ROW_CHUNKS, 3)), dma((ROW_CHUNKS, 3)),
            dma((2, 2, RING_CHUNKS)), dma((RING_CHUNKS,)), dma((2, 2, RING_CHUNKS)),
            dma((2,)), dma((2,)),
            dma((4,)), dma((4,)),
            dma((4, 15)), dma((4,)),
            dma((4, 7)), dma((4,)),
            dma((4, 3)), dma((4, 3)),
            dma((4, 3)), dma((4, 3)),
            dma((4,)), dma((4,)),
        ],
        compiler_params=pltpu.CompilerParams(
            collective_id=0, has_side_effects=True, vmem_limit_bytes=56 << 20
        ),
        name="factor_corner_and_update",
    )(a)


def solution(mesh):
    return jax.shard_map(
        body,
        mesh=mesh,
        in_specs=(P("row", "col"),),
        out_specs=P("row", "col"),
        check_vma=False,
    )
```

```python
import functools

import jax
import jax.numpy as jnp
from jax import lax
from jax.experimental import pallas as pl
from jax.experimental.pallas import tpu as pltpu
from jax.sharding import PartitionSpec as P

NB = 256
SUBPANELS = 4
MESH = pl.DeviceIdType.MESH
F32 = jnp.float32
BF16 = jnp.bfloat16


def split3(x):
    high = x.astype(BF16)
    rest = x - high.astype(F32)
    middle = rest.astype(BF16)
    low = (rest - middle.astype(F32)).astype(BF16)
    return high, middle, low


def split2(x):
    high = x.astype(BF16)
    return high, (x - high.astype(F32)).astype(BF16)


def dot_nn(a, b):
    return lax.dot_general(a, b, (((1,), (0,)), ((), ())), preferred_element_type=F32)


def dot_nt(a, b):
    return lax.dot_general(a, b, (((1,), (1,)), ((), ())), preferred_element_type=F32)


def dot3(dot, a, b):
    return dot(a[0], b[0]) + (dot(a[0], b[1]) + dot(a[1], b[0]))


def tree_sum(terms):
    while len(terms) > 1:
        terms = [sum(terms[i + 1 : i + 2], terms[i]) for i in range(0, len(terms), 2)]
    return terms[0]


def eliminate(tiles, s, first, active, iota):
    quarter, lane = divmod(first, 128)

    def spread(x):
        return jnp.broadcast_to(x, (8, 128))

    column = {
        t: [spread(tiles[t][quarter][:, lane + k : lane + k + 1]) for k in range(8)]
        for t in range(s, 4)
    }
    e = [[spread(column[s][k][i : i + 1, :]) if k <= i else None for k in range(8)] for i in range(8)]
    low = [[None] * 8 for _ in range(8)]
    inv = [[None] * 8 for _ in range(8)]
    for j in range(8):
        root = lax.rsqrt(e[j][j])
        for i in range(j + 1, 8):
            low[i][j] = e[i][j] * root
        for i in range(j + 1, 8):
            for k in range(j + 1, i + 1):
                e[i][k] = e[i][k] - low[i][j] * low[k][j]
        inv[j][j] = root
        for k in range(j):
            total = low[j][k] * inv[k][k]
            for m in range(k + 1, j):
                total = total + low[j][m] * inv[m][k]
            inv[j][k] = -(root * total)
    columns = []
    for k in range(8):
        value = inv[7][k]
        for i in range(6, k - 1, -1):
            value = jnp.where(iota == i, inv[i][k], value)
        if k > 0:
            value = jnp.where(iota < k, 0.0, value)
        columns.append(value)
    done = {
        q: tree_sum([columns[k] * spread(tiles[s][q][k : k + 1, :]) for k in range(8)])
        for q in active
    }
    for t in range(s + 1, 4):
        factor = [tree_sum([column[t][m] * inv[k][m] for m in range(k + 1)]) for k in range(8)]
        for q in active:
            tiles[t][q] = tiles[t][q] - tree_sum(
                [factor[k] * spread(done[q][k : k + 1, :]) for k in range(8)]
            )
    tiles[s].update(done)


def factor_block(work):
    iota = lax.broadcasted_iota(jnp.int32, (8, 128), 0)
    for slab in range(8):
        first = 32 * slab
        active = [0, 1, 2] if slab < 4 else [1, 2, 3]
        tiles = [
            {q: work[first + 8 * t : first + 8 * t + 8, 128 * q : 128 * q + 128] for q in active}
            for t in range(4)
        ]
        for s in range(4):
            eliminate(tiles, s, first + 8 * s, active, iota)
        for t in range(4):
            for q in active:
                work[first + 8 * t : first + 8 * t + 8, 128 * q : 128 * q + 128] = tiles[t][q]
        if slab == 7:
            break
        left = 128 * active[0]
        top = jnp.concatenate(
            [jnp.concatenate([tiles[t][q] for q in active], axis=1) for t in range(4)], axis=0
        )
        high, middle, low = split3(top)
        right = jnp.concatenate([high, middle, high, middle, low, high], axis=0)
        across = top[:, : 256 - left].T
        high, middle, low = split3(across)
        down = jnp.concatenate([high, high, middle, middle, high, low], axis=1)
        for begin, end in ((first + 32, first + 64), (first + 64, 256)):
            if begin < end:
                work[begin:end, left : left + 384] = work[begin:end, left : left + 384] - dot_nn(
                    down[begin - left : end - left], right
                )


ROW_CHUNKS = 6
RING_CHUNKS = 16
RING_LAG = 3
RING_STEPS = RING_CHUNKS + 5 * RING_LAG + 1


def factor_kernel(
    a_ref, o_ref,
    rows, cols, low, corner, work, p2, v2, column,
    local, c_send, c_recv, x_send, x_recv, y_send, y_recv, y_next, z_send, z_extra, z_recv,
    q_send, q_recv, r_send, r_recv, s_send, s_recv, t_send, t_recv,
    u_send, u_recv, w_send, w_recv, e_send, e_recv,
):
    size = a_ref.shape[0]
    row, col = lax.axis_index("row"), lax.axis_index("col")
    z, core = row // 2, row % 2
    x, y = col // 4, col % 4
    both, either, no = jnp.logical_and, jnp.logical_or, jnp.logical_not
    is_root = both(row == 0, col == 0)
    is_spreader = both(row == 1, col == 0)
    root, spreader = (0, 0), (1, 0)

    def at(zz, cc, xx, yy):
        return (zz * 2 + cc, xx * 4 + yy)

    def ring(step):
        return at((z + step) % 8, core, x, y)

    def plane(dx, dy):
        return at(z, core, (x + dx) % 4, (y + dy) % 4)

    pair = at(z, 1 - core, x, y)

    def remote(ref, send, recv, where, src=None):
        return pltpu.make_async_remote_copy(
            src_ref=ref if src is None else src, dst_ref=ref, send_sem=send, recv_sem=recv,
            device_id=where, device_id_type=MESH,
        )

    barrier = pltpu.get_barrier_semaphore()
    offsets = [(dx, dy) for dx in range(4) for dy in range(4) if dx or dy]
    peers = [ring(step) for step in range(1, 8)] + [plane(*o) for o in offsets] + [pair]
    for peer in peers:
        pl.semaphore_signal(barrier, inc=1, device_id=peer, device_id_type=MESH)
    owners = [(i, j) for i in range(SUBPANELS) for j in range(i + 1) if i or j]
    owner = both(both(row < SUBPANELS, col <= row), no(is_root))

    @pl.when(owner)
    def _():
        pl.semaphore_signal(barrier, inc=1, device_id=root, device_id_type=MESH)

    @pl.when(is_root)
    def _():
        for peer in owners:
            pl.semaphore_signal(barrier, inc=1, device_id=peer, device_id_type=MESH)

    keep = pltpu.make_async_copy(a_ref, o_ref, local.at[0])
    keep.start()
    own_cols = pltpu.make_async_copy(a_ref.at[0:NB, :], cols.at[row % SUBPANELS], local.at[1])
    own_rows = pltpu.make_async_copy(a_ref.at[:, 0:NB], rows.at[y], local.at[2])
    own_corner = pltpu.make_async_copy(a_ref.at[0:NB, 0:NB], corner.at[0, 0], local.at[3])
    pl.when(row < SUBPANELS)(own_cols.start)
    pl.when(x == 0)(own_rows.start)
    pl.when(is_root)(own_corner.start)
    total = len(peers) + jnp.where(owner, 1, 0) + jnp.where(is_root, len(owners), 0)
    pl.semaphore_wait(barrier, total)

    def corner_copy(i, j):
        return remote(
            corner.at[i, j], c_send.at[0], c_recv.at[i * SUBPANELS + j], root,
            src=a_ref.at[0:NB, 0:NB],
        )

    for i, j in owners:
        pl.when(both(row == i, col == j))(corner_copy(i, j).start)
    pl.when(row < SUBPANELS)(own_cols.wait)
    pl.when(x == 0)(own_rows.wait)

    def row_ref(source, chunk):
        length = size // ROW_CHUNKS
        return rows.at[source, chunk * length : (chunk + 1) * length, :]

    def row_half(source, chunk, part):
        length = size // ROW_CHUNKS // 2
        begin = (2 * chunk + part) * length
        return rows.at[source, begin : begin + length, :]

    def x_copy(chunk, side):
        return remote(
            row_ref(y, chunk), x_send.at[chunk, side], x_recv.at[chunk, 0], plane(1 + 2 * side, 0)
        )

    def x_half(chunk, side):
        return remote(
            row_half(y, chunk, side), x_send.at[chunk, 0], x_recv.at[chunk, side],
            plane(1 + 2 * side, 0),
        )

    beside_root = both(both(x == 0, z == 0), core == 0)
    direct = both(beside_root, y % 2 == 1)
    passing = no(both(beside_root, y % 2 == 0))

    def y_copy(chunk, side):
        return remote(
            row_ref(y, chunk), y_send.at[chunk, side], y_recv.at[chunk, side],
            plane(0, 1 + 2 * side),
        )

    def y_direct(chunk, source):
        return remote(
            row_ref(source, chunk), y_send.at[chunk, 4], y_next.at[chunk, 0], plane(0, 2)
        )

    def y_arrival(chunk, side):
        return remote(
            row_ref((y + 3 + 2 * side) % 4, chunk), y_send.at[chunk, side], y_recv.at[chunk, side],
            pair,
        )

    def y_half(chunk, side, source):
        return remote(
            row_half(source, chunk, side), y_send.at[chunk, 2 + side], y_next.at[chunk, side],
            plane(0, 1 + 2 * side),
        )

    def y_start(chunk):
        for side in range(2):
            y_copy(chunk, side).start()
        pl.when(direct)(y_direct(chunk, y).start)

    def row_step(chunk):
        for side in range(2):
            @pl.when(x == 1 + 2 * side)
            def _():
                x_copy(chunk, 0).wait_recv()
                x_half(chunk, side).start()

        @pl.when(x == 2)
        def _():
            for side in range(2):
                x_half(chunk, side).wait_recv()

        pl.when(x != 0)(lambda: y_start(chunk))

    def row_pass(chunk):
        for side in range(2):
            y_arrival(chunk, side).wait_recv()

            @pl.when(passing)
            def _():
                y_half(chunk, side, (y + 3 + 2 * side) % 4).start()

    def row_last(chunk):
        @pl.when(direct)
        def _():
            y_direct(chunk, (y + 2) % 4).wait_recv()

        @pl.when(no(direct))
        def _():
            for side in range(2):
                y_half(chunk, side, (y + 2) % 4).wait_recv()

    def rows_sent():
        for chunk in range(ROW_CHUNKS):
            for side in range(2):
                pl.when(x == 0)(x_copy(chunk, side).wait_send)
                pl.when(x == 1 + 2 * side)(x_half(chunk, side).wait_send)
                y_copy(chunk, side).wait_send()
                pl.when(passing)(y_half(chunk, side, y).wait_send)
            pl.when(direct)(y_direct(chunk, y).wait_send)

    def ring_ref(u, way, chunk):
        length = NB // 2 // RING_CHUNKS
        begin = pl.multiple_of(way * (NB // 2) + chunk * length, length)
        return cols.at[2 * u + core, pl.ds(begin, length), :]

    def distance(u, way):
        return (z - u + 8) % 8 if way == 0 else (u - z + 8) % 8

    def ring_copy(u, way, chunk):
        step = 1 if way == 0 else 7
        if (u, way) == (1, 1):
            where = at(jnp.where(z == 1, 7, (z + 7) % 8), core, x, y)
        else:
            where = ring(step)
        return remote(
            ring_ref(u, way, chunk), z_send.at[u, way, chunk], z_recv.at[u, way, chunk], where
        )

    def ring_second(chunk):
        return remote(ring_ref(1, 1, chunk), z_extra.at[chunk], z_recv.at[1, 1, chunk], ring(7))

    def ring_passes(u, way):
        passes = distance(u, way) < 7
        return both(passes, z != 0) if (u, way) == (1, 1) else passes

    def each_chunk(action):
        def one(chunk, _):
            action(chunk)
            return 0

        lax.fori_loop(0, RING_CHUNKS, one, 0)

    def slab_copy(u, which):
        return remote(cols.at[2 * u + which], q_send.at[u], q_recv.at[u], pair)

    @pl.when(x == 0)
    def _():
        for chunk in range(ROW_CHUNKS):
            for side in range(2):
                x_copy(chunk, side).start()
            y_start(chunk)

    def ring_start(chunk):
        for u in range(2):
            @pl.when(z == u)
            def _():
                for way in range(2):
                    ring_copy(u, way, chunk).start()
                if u == 1:
                    ring_second(chunk).start()

    each_chunk(ring_start)

    def group(k, begin, length):
        return low.at[k, 0 : SUBPANELS - k, pl.ds(begin, length), :]

    def give(k):
        return remote(group(k, 0, NB), r_send.at[k], r_recv.at[k], spreader)

    def deal(k, dx, dy):
        piece = (4 * dy + dx) * 16
        return remote(
            group(k, piece, 16), s_send.at[k, 4 * dx + dy - 1], s_recv.at[k], (1, dx * 4 + dy)
        )

    mine = pl.multiple_of((4 * y + x) * 16, 16)

    def climb(k, step):
        return remote(group(k, mine, 16), t_send.at[k, step - 1], t_recv.at[k], ring(step))

    def spread_x(k, d):
        return remote(group(k, mine, 16), u_send.at[k, d - 1], u_recv.at[k, d - 1], plane(d, 0))

    def spread_x_arrival(k, d):
        begin = pl.multiple_of((4 * y + (x + 4 - d) % 4) * 16, 16)
        return remote(group(k, begin, 16), u_send.at[k, d - 1], u_recv.at[k, d - 1], pair)

    def spread_y(k, d):
        begin = pl.multiple_of(y * 64, 64)
        return remote(group(k, begin, 64), w_send.at[k, d - 1], w_recv.at[k, d - 1], plane(0, d))

    def spread_y_arrival(k, d):
        begin = pl.multiple_of((y + 4 - d) % 4 * 64, 64)
        return remote(group(k, begin, 64), w_send.at[k, d - 1], w_recv.at[k, d - 1], pair)

    def to_pair(k):
        return remote(group(k, 0, NB), e_send.at[k], e_recv.at[k], pair)

    def x_goes(d):
        return both(core == 1, no(both(both(z == 0, y == 0), (x + d) % 4 == 0)))

    def y_goes(d):
        return both(core == 1, no(both(both(z == 0, x == 0), (y + d) % 4 == 0)))

    takes = both(core == 1, no(is_spreader))

    def stage1(k):
        @pl.when(is_spreader)
        def _():
            give(k).wait_recv()
            for dx, dy in offsets:
                deal(k, dx, dy).start()

    def stage2(k):
        @pl.when(both(core == 1, z == 0))
        def _():
            @pl.when(no(is_spreader))
            def _():
                remote(group(k, mine, 16), r_send.at[k], s_recv.at[k], pair).wait_recv()

            for step in range(1, 8):
                climb(k, step).start()

    def stage3(k):
        @pl.when(both(core == 1, z != 0))
        def _():
            climb(k, 1).wait_recv()

        for d in range(1, 4):
            pl.when(x_goes(d))(spread_x(k, d).start)

    def stage4(k):
        @pl.when(takes)
        def _():
            for d in range(1, 4):
                spread_x_arrival(k, d).wait_recv()

        for d in range(1, 4):
            pl.when(y_goes(d))(spread_y(k, d).start)

    def stage5(k):
        @pl.when(takes)
        def _():
            for d in range(1, 4):
                spread_y_arrival(k, d).wait_recv()
            to_pair(k).start()

        @pl.when(both(core == 0, no(is_root)))
        def _():
            to_pair(k).wait_recv()

    def group_sent(k):
        pl.when(is_root)(give(k).wait_send)

        @pl.when(is_spreader)
        def _():
            for dx, dy in offsets:
                deal(k, dx, dy).wait_send()

        @pl.when(both(core == 1, z == 0))
        def _():
            for step in range(1, 8):
                climb(k, step).wait_send()

        for d in range(1, 4):
            pl.when(x_goes(d))(spread_x(k, d).wait_send)
            pl.when(y_goes(d))(spread_y(k, d).wait_send)
        pl.when(takes)(to_pair(k).wait_send)

    iota_r = lax.broadcasted_iota(jnp.int32, (NB, NB), 0)
    iota_c = lax.broadcasted_iota(jnp.int32, (NB, NB), 1)

    def ring_step(n):
        for u in range(2):
            for way in range(2):
                away = distance(u, way)
                chunk = n - RING_LAG * (away - 1)

                @pl.when(
                    both(both(away > 0, ring_passes(u, way)), both(chunk >= 0, chunk < RING_CHUNKS))
                )
                def _():
                    copy = ring_copy(u, way, chunk)
                    copy.wait_recv()
                    copy.start()

    def ring_finish():
        for u in range(2):
            for way in range(2):
                @pl.when(both(distance(u, way) > 0, no(ring_passes(u, way))))
                def _():
                    each_chunk(lambda chunk: ring_copy(u, way, chunk).wait_recv())

            slab_copy(u, core).start()

    def slabs_arrived():
        for chunk in range(ROW_CHUNKS):
            row_last(chunk)
        for u in range(2):
            slab_copy(u, 1 - core).wait_recv()
        keep.wait()
        rows_sent()
        for u in range(2):
            for way in range(2):
                @pl.when(ring_passes(u, way))
                def _():
                    each_chunk(lambda chunk: ring_copy(u, way, chunk).wait_send())

            slab_copy(u, core).wait_send()
        pl.when(z == 1)(lambda: each_chunk(lambda chunk: ring_second(chunk).wait_send()))

    def update(k):
        inv = split2(low[k, 0])
        p = dot3(dot_nt, split2(rows[k]), inv)
        p2[0], p2[1] = split2(p)
        v2[0], v2[1] = split2(dot3(dot_nn, inv, split2(cols[k])))
        o_ref[...] = o_ref[...] - dot3(dot_nn, (p2[0], p2[1]), (v2[0], v2[1]))

        @pl.when(col == k)
        def _():
            column[...] = p

        def rest(m, _):
            block = split2(low[k, m - k])
            rows[m] = rows[m] - dot3(dot_nt, (p2[0], p2[1]), block)
            cols[m] = cols[m] - dot3(dot_nn, block, (v2[0], v2[1]))
            return 0

        lax.fori_loop(k + 1, SUBPANELS, rest, 0)

    @pl.when(is_root)
    def _():
        own_corner.wait()
        eye = jnp.where(iota_r == iota_c, 1.0, 0.0).astype(F32)

        def step(k, _):
            work[:, 0:NB] = corner[k, k]
            work[:, NB : 2 * NB] = eye
            factor_block(work)
            inverse = jnp.where(iota_r >= iota_c, work[:, NB : 2 * NB], 0.0)
            low[k, 0] = inverse
            inv = split2(inverse)

            @pl.when(k == 0)
            def _():
                for i, j in owners:
                    corner_copy(i, j).wait_recv()

            def below(i, _):
                low[k, i - k] = dot3(dot_nt, split2(corner[i, k]), inv)
                return 0

            lax.fori_loop(k + 1, SUBPANELS, below, 0)
            for fixed in range(SUBPANELS):
                pl.when(k == fixed)(give(fixed).start)

            def trail(i, _):
                def inner(j, _):
                    corner[i, j] = corner[i, j] - dot3(
                        dot_nt, split2(low[k, i - k]), split2(low[k, j - k])
                    )
                    return 0

                return lax.fori_loop(k + 1, i + 1, inner, 0)

            return lax.fori_loop(k + 1, SUBPANELS, trail, 0)

        lax.fori_loop(0, SUBPANELS, step, 0)
        ring_finish()
        for chunk in range(ROW_CHUNKS):
            row_pass(chunk)
        slabs_arrived()
        lax.fori_loop(0, SUBPANELS, lambda k, c: (update(k), c)[1], 0)

    @pl.when(no(is_root))
    def _():
        plan = {
            10: [(stage1, 0)], 16: [(stage2, 0)], 19: [(stage1, 1)], 22: [(stage3, 0)],
            26: [(stage2, 1), (stage4, 0)],
        }
        for chunk in range(ROW_CHUNKS):
            plan.setdefault(5 + 3 * chunk, []).append((row_step, chunk))
            plan.setdefault(8 + 4 * chunk, []).append((row_pass, chunk))

        def one(n, _):
            ring_step(n)
            for when, actions in plan.items():
                @pl.when(n == when)
                def _():
                    for action, argument in actions:
                        action(argument)

            return 0

        lax.fori_loop(0, RING_STEPS, one, 0)
        stage3(1)
        ring_finish()
        stage1(2)
        stage2(2)
        stage5(0)
        stage4(1)
        pl.when(is_spreader)(lambda: (stage3(2), stage4(2), stage1(3), stage2(3)) and None)
        slabs_arrived()

        def some(k, _):
            update(k)
            for fixed in range(SUBPANELS - 1):
                @pl.when(k == fixed)
                def _():
                    if fixed == 0:
                        pl.when(no(is_spreader))(lambda: stage3(2))
                        stage5(1)
                        pl.when(no(is_spreader))(lambda: (stage4(2), stage2(3)) and None)
                    if fixed == 1:
                        stage5(2)
                        stage3(3)
                    if fixed == 2:
                        stage4(3)
                        stage5(3)

            return 0

        lax.fori_loop(0, SUBPANELS, some, 0)

    top, left = row < SUBPANELS, col < SUBPANELS

    @pl.when(left)
    def _():
        o_ref[:, 0:NB] = column[...]

    @pl.when(top)
    def _():
        o_ref[0:NB, NB:] = jnp.zeros((NB, size - NB), F32)

    @pl.when(both(top, col > row))
    def _():
        o_ref[0:NB, 0:NB] = jnp.zeros((NB, NB), F32)

    @pl.when(both(top, col == row))
    def _():
        o_ref[0:NB, 0:NB] = jnp.where(iota_r >= iota_c, o_ref[0:NB, 0:NB], 0.0)

    pl.when(owner)(corner_copy(0, 0).wait_send)

    for k in range(SUBPANELS):
        group_sent(k)


def body(a):
    size = a.shape[0]
    dma = pltpu.SemaphoreType.DMA
    vmem = pltpu.VMEM
    return pl.pallas_call(
        factor_kernel,
        out_shape=jax.ShapeDtypeStruct(a.shape, F32),
        in_specs=[pl.BlockSpec(memory_space=pl.ANY)],
        out_specs=pl.BlockSpec(memory_space=pltpu.VMEM),
        scratch_shapes=[
            vmem((SUBPANELS, size, NB), F32),
            vmem((SUBPANELS, NB, size), F32),
            vmem((SUBPANELS, SUBPANELS, NB, NB), F32),
            vmem((SUBPANELS, SUBPANELS, NB, NB), F32),
            vmem((NB, 2 * NB), F32),
            vmem((2, size, NB), BF16),
            vmem((2, NB, size), BF16),
            vmem((size, NB), F32),
            dma((4,)),
            dma((1,)), dma((16,)),
            dma((ROW_CHUNKS, 2)), dma((ROW_CHUNKS, 2)),
            dma((ROW_CHUNKS, 5)), dma((ROW_CHUNKS, 2)), dma((ROW_CHUNKS, 2)),
            dma((2, 2, RING_CHUNKS)), dma((RING_CHUNKS,)), dma((2, 2, RING_CHUNKS)),
            dma((2,)), dma((2,)),
            dma((4,)), dma((4,)),
            dma((4, 15)), dma((4,)),
            dma((4, 7)), dma((4,)),
            dma((4, 3)), dma((4, 3)),
            dma((4, 3)), dma((4, 3)),
            dma((4,)), dma((4,)),
        ],
        compiler_params=pltpu.CompilerParams(
            collective_id=0, has_side_effects=True, vmem_limit_bytes=56 << 20
        ),
        name="factor_corner_and_update",
    )(a)


def solution(mesh):
    return jax.shard_map(
        body,
        mesh=mesh,
        in_specs=(P("row", "col"),),
        out_specs=P("row", "col"),
        check_vma=False,
    )
```

```python
import functools

import jax
import jax.numpy as jnp
from jax import lax
from jax.experimental import pallas as pl
from jax.experimental.pallas import tpu as pltpu
from jax.sharding import PartitionSpec as P

NB = 256
SUBPANELS = 4
MESH = pl.DeviceIdType.MESH
F32 = jnp.float32
BF16 = jnp.bfloat16


def split3(x):
    high = x.astype(BF16)
    rest = x - high.astype(F32)
    middle = rest.astype(BF16)
    low = (rest - middle.astype(F32)).astype(BF16)
    return high, middle, low


def split2(x):
    high = x.astype(BF16)
    return high, (x - high.astype(F32)).astype(BF16)


def dot_nn(a, b):
    return lax.dot_general(a, b, (((1,), (0,)), ((), ())), preferred_element_type=F32)


def dot_nt(a, b):
    return lax.dot_general(a, b, (((1,), (1,)), ((), ())), preferred_element_type=F32)


def dot3(dot, a, b):
    return dot(a[0], b[0]) + (dot(a[0], b[1]) + dot(a[1], b[0]))


def tree_sum(terms):
    while len(terms) > 1:
        terms = [sum(terms[i + 1 : i + 2], terms[i]) for i in range(0, len(terms), 2)]
    return terms[0]


def eliminate(tiles, s, first, active, iota):
    quarter, lane = divmod(first, 128)

    def spread(x):
        return jnp.broadcast_to(x, (8, 128))

    column = {
        t: [spread(tiles[t][quarter][:, lane + k : lane + k + 1]) for k in range(8)]
        for t in range(s, 4)
    }
    e = [[spread(column[s][k][i : i + 1, :]) if k <= i else None for k in range(8)] for i in range(8)]
    low = [[None] * 8 for _ in range(8)]
    inv = [[None] * 8 for _ in range(8)]
    for j in range(8):
        root = lax.rsqrt(e[j][j])
        for i in range(j + 1, 8):
            low[i][j] = e[i][j] * root
        for i in range(j + 1, 8):
            for k in range(j + 1, i + 1):
                e[i][k] = e[i][k] - low[i][j] * low[k][j]
        inv[j][j] = root
        for k in range(j):
            total = low[j][k] * inv[k][k]
            for m in range(k + 1, j):
                total = total + low[j][m] * inv[m][k]
            inv[j][k] = -(root * total)
    columns = []
    for k in range(8):
        value = inv[7][k]
        for i in range(6, k - 1, -1):
            value = jnp.where(iota == i, inv[i][k], value)
        if k > 0:
            value = jnp.where(iota < k, 0.0, value)
        columns.append(value)
    done = {
        q: tree_sum([columns[k] * spread(tiles[s][q][k : k + 1, :]) for k in range(8)])
        for q in active
    }
    for t in range(s + 1, 4):
        factor = [tree_sum([column[t][m] * inv[k][m] for m in range(k + 1)]) for k in range(8)]
        for q in active:
            tiles[t][q] = tiles[t][q] - tree_sum(
                [factor[k] * spread(done[q][k : k + 1, :]) for k in range(8)]
            )
    tiles[s].update(done)


def factor_block(work):
    iota = lax.broadcasted_iota(jnp.int32, (8, 128), 0)
    for slab in range(8):
        first = 32 * slab
        active = [0, 1, 2] if slab < 4 else [1, 2, 3]
        tiles = [
            {q: work[first + 8 * t : first + 8 * t + 8, 128 * q : 128 * q + 128] for q in active}
            for t in range(4)
        ]
        for s in range(4):
            eliminate(tiles, s, first + 8 * s, active, iota)
        for t in range(4):
            for q in active:
                work[first + 8 * t : first + 8 * t + 8, 128 * q : 128 * q + 128] = tiles[t][q]
        if slab == 7:
            break
        left = 128 * active[0]
        top = jnp.concatenate(
            [jnp.concatenate([tiles[t][q] for q in active], axis=1) for t in range(4)], axis=0
        )
        high, middle, low = split3(top)
        right = jnp.concatenate([high, middle, high, middle, low, high], axis=0)
        across = top[:, : 256 - left].T
        high, middle, low = split3(across)
        down = jnp.concatenate([high, high, middle, middle, high, low], axis=1)
        for begin, end in ((first + 32, first + 64), (first + 64, 256)):
            if begin < end:
                work[begin:end, left : left + 384] = work[begin:end, left : left + 384] - dot_nn(
                    down[begin - left : end - left], right
                )


ROW_CHUNKS = 6
RING_CHUNKS = 16
RING_LAG = 3
AHEAD = 2
RING_STEPS = max(RING_CHUNKS + 5 * RING_LAG, 9 + 4 * (ROW_CHUNKS - 1))


def factor_kernel(
    a_ref, o_ref,
    rows, cols, low, corner, work, p2, v2, column,
    local, c_send, c_recv, x_send, x_recv, y_send, y_recv, y_next, z_send, z_extra, z_recv,
    q_send, q_recv, r_send, r_recv, s_send, s_recv, t_send, t_recv,
    u_send, u_recv, w_send, w_recv, e_send, e_recv,
):
    size = a_ref.shape[0]
    row, col = lax.axis_index("row"), lax.axis_index("col")
    z, core = row // 2, row % 2
    x, y = col // 4, col % 4
    both, either, no = jnp.logical_and, jnp.logical_or, jnp.logical_not
    is_root = both(row == 0, col == 0)
    is_spreader = both(row == 1, col == 0)
    root, spreader = (0, 0), (1, 0)

    def at(zz, cc, xx, yy):
        return (zz * 2 + cc, xx * 4 + yy)

    def ring(step):
        return at((z + step) % 8, core, x, y)

    def plane(dx, dy):
        return at(z, core, (x + dx) % 4, (y + dy) % 4)

    pair = at(z, 1 - core, x, y)

    def remote(ref, send, recv, where, src=None):
        return pltpu.make_async_remote_copy(
            src_ref=ref if src is None else src, dst_ref=ref, send_sem=send, recv_sem=recv,
            device_id=where, device_id_type=MESH,
        )

    barrier = pltpu.get_barrier_semaphore()
    offsets = [(dx, dy) for dx in range(4) for dy in range(4) if dx or dy]
    peers = [ring(step) for step in range(1, 8)] + [plane(*o) for o in offsets] + [pair]
    for peer in peers:
        pl.semaphore_signal(barrier, inc=1, device_id=peer, device_id_type=MESH)
    owners = [(i, j) for i in range(SUBPANELS) for j in range(i + 1) if i or j]
    owner = both(both(row < SUBPANELS, col <= row), no(is_root))

    @pl.when(owner)
    def _():
        pl.semaphore_signal(barrier, inc=1, device_id=root, device_id_type=MESH)

    @pl.when(is_root)
    def _():
        for peer in owners:
            pl.semaphore_signal(barrier, inc=1, device_id=peer, device_id_type=MESH)

    keep = pltpu.make_async_copy(a_ref, o_ref, local.at[0])
    keep.start()
    own_cols = pltpu.make_async_copy(a_ref.at[0:NB, :], cols.at[row % SUBPANELS], local.at[1])
    own_rows = pltpu.make_async_copy(a_ref.at[:, 0:NB], rows.at[y], local.at[2])
    own_corner = pltpu.make_async_copy(a_ref.at[0:NB, 0:NB], corner.at[0, 0], local.at[3])
    pl.when(row < SUBPANELS)(own_cols.start)
    pl.when(x == 0)(own_rows.start)
    pl.when(is_root)(own_corner.start)
    total = len(peers) + jnp.where(owner, 1, 0) + jnp.where(is_root, len(owners), 0)
    pl.semaphore_wait(barrier, total)

    def corner_copy(i, j):
        return remote(
            corner.at[i, j], c_send.at[0], c_recv.at[i * SUBPANELS + j], root,
            src=a_ref.at[0:NB, 0:NB],
        )

    for i, j in owners:
        pl.when(both(row == i, col == j))(corner_copy(i, j).start)
    pl.when(row < SUBPANELS)(own_cols.wait)
    pl.when(x == 0)(own_rows.wait)

    def row_ref(source, chunk):
        length = size // ROW_CHUNKS
        return rows.at[source, chunk * length : (chunk + 1) * length, :]

    def row_half(source, chunk, part):
        length = size // ROW_CHUNKS // 2
        begin = (2 * chunk + part) * length
        return rows.at[source, begin : begin + length, :]

    def x_copy(chunk, side):
        return remote(
            row_ref(y, chunk), x_send.at[chunk, side], x_recv.at[chunk, 0], plane(1 + 2 * side, 0)
        )

    def x_half(chunk, side):
        return remote(
            row_half(y, chunk, side), x_send.at[chunk, 0], x_recv.at[chunk, side],
            plane(1 + 2 * side, 0),
        )

    beside_root = both(both(x == 0, z == 0), core == 0)
    direct = both(beside_root, y % 2 == 1)
    passing = no(both(beside_root, y % 2 == 0))

    def y_copy(chunk, side):
        return remote(
            row_ref(y, chunk), y_send.at[chunk, side], y_recv.at[chunk, side],
            plane(0, 1 + 2 * side),
        )

    def y_direct(chunk, source):
        return remote(
            row_ref(source, chunk), y_send.at[chunk, 4], y_next.at[chunk, 0], plane(0, 2)
        )

    def y_arrival(chunk, side):
        return remote(
            row_ref((y + 3 + 2 * side) % 4, chunk), y_send.at[chunk, side], y_recv.at[chunk, side],
            pair,
        )

    def y_half(chunk, side, source):
        return remote(
            row_half(source, chunk, side), y_send.at[chunk, 2 + side], y_next.at[chunk, side],
            plane(0, 1 + 2 * side),
        )

    def y_start(chunk):
        for side in range(2):
            y_copy(chunk, side).start()
        pl.when(direct)(y_direct(chunk, y).start)

    def row_first(chunk):
        pl.when(x == 0)(lambda: first_start(chunk))

    def row_step(chunk):
        for side in range(2):
            @pl.when(x == 1 + 2 * side)
            def _():
                x_copy(chunk, 0).wait_recv()
                x_half(chunk, side).start()

        @pl.when(x == 2)
        def _():
            for side in range(2):
                x_half(chunk, side).wait_recv()

        pl.when(x != 0)(lambda: y_start(chunk))

    def row_pass(chunk):
        for side in range(2):
            y_arrival(chunk, side).wait_recv()

            @pl.when(passing)
            def _():
                y_half(chunk, side, (y + 3 + 2 * side) % 4).start()

    def row_last(chunk):
        @pl.when(direct)
        def _():
            y_direct(chunk, (y + 2) % 4).wait_recv()

        @pl.when(no(direct))
        def _():
            for side in range(2):
                y_half(chunk, side, (y + 2) % 4).wait_recv()

    def rows_sent():
        for chunk in range(ROW_CHUNKS):
            for side in range(2):
                pl.when(x == 0)(x_copy(chunk, side).wait_send)
                pl.when(x == 1 + 2 * side)(x_half(chunk, side).wait_send)
                y_copy(chunk, side).wait_send()
                pl.when(passing)(y_half(chunk, side, y).wait_send)
            pl.when(direct)(y_direct(chunk, y).wait_send)

    def ring_ref(u, way, chunk):
        length = NB // 2 // RING_CHUNKS
        begin = pl.multiple_of(way * (NB // 2) + chunk * length, length)
        return cols.at[2 * u + core, pl.ds(begin, length), :]

    def distance(u, way):
        return (z - u + 8) % 8 if way == 0 else (u - z + 8) % 8

    def ring_copy(u, way, chunk):
        step = 1 if way == 0 else 7
        if (u, way) == (1, 1):
            where = at(jnp.where(z == 1, 7, (z + 7) % 8), core, x, y)
        else:
            where = ring(step)
        return remote(
            ring_ref(u, way, chunk), z_send.at[u, way, chunk], z_recv.at[u, way, chunk], where
        )

    def ring_second(chunk):
        return remote(ring_ref(1, 1, chunk), z_extra.at[chunk], z_recv.at[1, 1, chunk], ring(7))

    def ring_passes(u, way):
        passes = distance(u, way) < 7
        return both(passes, z != 0) if (u, way) == (1, 1) else passes

    def each_chunk(action):
        def one(chunk, _):
            action(chunk)
            return 0

        lax.fori_loop(0, RING_CHUNKS, one, 0)

    def slab_copy(u, which):
        return remote(cols.at[2 * u + which], q_send.at[u], q_recv.at[u], pair)

    def first_start(chunk):
        for side in range(2):
            x_copy(chunk, side).start()
        y_start(chunk)

    def ring_source(u, chunk, action):
        for way in range(2):
            action(ring_copy(u, way, chunk))
        if u == 1:
            action(ring_second(chunk))

    @pl.when(is_root)
    def _():
        for chunk in range(ROW_CHUNKS):
            first_start(chunk)
        each_chunk(lambda chunk: ring_source(0, chunk, lambda copy: copy.start()))

    def group(k, begin, length):
        return low.at[k, 0 : SUBPANELS - k, pl.ds(begin, length), :]

    def give(k):
        return remote(group(k, 0, NB), r_send.at[k], r_recv.at[k], spreader)

    def deal(k, dx, dy):
        piece = (4 * dy + dx) * 16
        return remote(
            group(k, piece, 16), s_send.at[k, 4 * dx + dy - 1], s_recv.at[k], (1, dx * 4 + dy)
        )

    mine = pl.multiple_of((4 * y + x) * 16, 16)

    def climb(k, step):
        return remote(group(k, mine, 16), t_send.at[k, step - 1], t_recv.at[k], ring(step))

    def spread_x(k, d):
        return remote(group(k, mine, 16), u_send.at[k, d - 1], u_recv.at[k, d - 1], plane(d, 0))

    def spread_x_arrival(k, d):
        begin = pl.multiple_of((4 * y + (x + 4 - d) % 4) * 16, 16)
        return remote(group(k, begin, 16), u_send.at[k, d - 1], u_recv.at[k, d - 1], pair)

    def spread_y(k, d):
        begin = pl.multiple_of(y * 64, 64)
        return remote(group(k, begin, 64), w_send.at[k, d - 1], w_recv.at[k, d - 1], plane(0, d))

    def spread_y_arrival(k, d):
        begin = pl.multiple_of((y + 4 - d) % 4 * 64, 64)
        return remote(group(k, begin, 64), w_send.at[k, d - 1], w_recv.at[k, d - 1], pair)

    def to_pair(k):
        return remote(group(k, 0, NB), e_send.at[k], e_recv.at[k], pair)

    def x_goes(d):
        return both(core == 1, no(both(both(z == 0, y == 0), (x + d) % 4 == 0)))

    def y_goes(d):
        return both(core == 1, no(both(both(z == 0, x == 0), (y + d) % 4 == 0)))

    takes = both(core == 1, no(is_spreader))

    def stage1(k):
        @pl.when(is_spreader)
        def _():
            give(k).wait_recv()
            for dx, dy in offsets:
                deal(k, dx, dy).start()

    def stage2(k):
        @pl.when(both(core == 1, z == 0))
        def _():
            @pl.when(no(is_spreader))
            def _():
                remote(group(k, mine, 16), r_send.at[k], s_recv.at[k], pair).wait_recv()

            for step in range(1, 8):
                climb(k, step).start()

    def stage3(k):
        @pl.when(both(core == 1, z != 0))
        def _():
            climb(k, 1).wait_recv()

        for d in range(1, 4):
            pl.when(x_goes(d))(spread_x(k, d).start)

    def stage4(k):
        @pl.when(takes)
        def _():
            for d in range(1, 4):
                spread_x_arrival(k, d).wait_recv()

        for d in range(1, 4):
            pl.when(y_goes(d))(spread_y(k, d).start)

    def stage5(k):
        @pl.when(takes)
        def _():
            for d in range(1, 4):
                spread_y_arrival(k, d).wait_recv()
            to_pair(k).start()

        @pl.when(both(core == 0, no(is_root)))
        def _():
            to_pair(k).wait_recv()

    def group_sent(k):
        pl.when(is_root)(give(k).wait_send)

        @pl.when(is_spreader)
        def _():
            for dx, dy in offsets:
                deal(k, dx, dy).wait_send()

        @pl.when(both(core == 1, z == 0))
        def _():
            for step in range(1, 8):
                climb(k, step).wait_send()

        for d in range(1, 4):
            pl.when(x_goes(d))(spread_x(k, d).wait_send)
            pl.when(y_goes(d))(spread_y(k, d).wait_send)
        pl.when(takes)(to_pair(k).wait_send)

    iota_r = lax.broadcasted_iota(jnp.int32, (NB, NB), 0)
    iota_c = lax.broadcasted_iota(jnp.int32, (NB, NB), 1)

    def ring_step(n):
        for u in range(2):
            @pl.when(both(z == u, n < RING_CHUNKS))
            def _():
                @pl.when(n >= AHEAD)
                def _():
                    ring_source(u, n - AHEAD, lambda copy: copy.wait_send())

                ring_source(u, n, lambda copy: copy.start())

        for u in range(2):
            for way in range(2):
                away = distance(u, way)
                chunk = n - RING_LAG * (away - 1)

                @pl.when(
                    both(both(away > 0, ring_passes(u, way)), both(chunk >= 0, chunk < RING_CHUNKS))
                )
                def _():
                    copy = ring_copy(u, way, chunk)
                    copy.wait_recv()
                    copy.start()

    def ring_finish():
        for u in range(2):
            for way in range(2):
                @pl.when(both(distance(u, way) > 0, no(ring_passes(u, way))))
                def _():
                    each_chunk(lambda chunk: ring_copy(u, way, chunk).wait_recv())

            slab_copy(u, core).start()

    def slabs_arrived():
        for chunk in range(ROW_CHUNKS):
            row_last(chunk)
        for u in range(2):
            slab_copy(u, 1 - core).wait_recv()
        keep.wait()
        rows_sent()
        for u in range(2):
            def left(chunk):
                @pl.when(both(z == u, either(is_root, chunk >= RING_CHUNKS - AHEAD)))
                def _():
                    ring_source(u, chunk, lambda copy: copy.wait_send())

                for way in range(2):
                    @pl.when(both(z != u, ring_passes(u, way)))
                    def _():
                        ring_copy(u, way, chunk).wait_send()

            each_chunk(left)
            slab_copy(u, core).wait_send()

    def update(k):
        inv = split2(low[k, 0])
        p = dot3(dot_nt, split2(rows[k]), inv)
        p2[0], p2[1] = split2(p)
        v2[0], v2[1] = split2(dot3(dot_nn, inv, split2(cols[k])))
        o_ref[...] = o_ref[...] - dot3(dot_nn, (p2[0], p2[1]), (v2[0], v2[1]))

        @pl.when(col == k)
        def _():
            column[...] = p

        def rest(m, _):
            block = split2(low[k, m - k])
            rows[m] = rows[m] - dot3(dot_nt, (p2[0], p2[1]), block)
            cols[m] = cols[m] - dot3(dot_nn, block, (v2[0], v2[1]))
            return 0

        lax.fori_loop(k + 1, SUBPANELS, rest, 0)

    @pl.when(is_root)
    def _():
        own_corner.wait()
        eye = jnp.where(iota_r == iota_c, 1.0, 0.0).astype(F32)

        def step(k, _):
            work[:, 0:NB] = corner[k, k]
            work[:, NB : 2 * NB] = eye
            factor_block(work)
            inverse = jnp.where(iota_r >= iota_c, work[:, NB : 2 * NB], 0.0)
            low[k, 0] = inverse
            inv = split2(inverse)

            @pl.when(k == 0)
            def _():
                for i, j in owners:
                    corner_copy(i, j).wait_recv()

            def below(i, _):
                low[k, i - k] = dot3(dot_nt, split2(corner[i, k]), inv)
                return 0

            lax.fori_loop(k + 1, SUBPANELS, below, 0)
            for fixed in range(SUBPANELS):
                pl.when(k == fixed)(give(fixed).start)

            def trail(i, _):
                def inner(j, _):
                    corner[i, j] = corner[i, j] - dot3(
                        dot_nt, split2(low[k, i - k]), split2(low[k, j - k])
                    )
                    return 0

                return lax.fori_loop(k + 1, i + 1, inner, 0)

            return lax.fori_loop(k + 1, SUBPANELS, trail, 0)

        lax.fori_loop(0, SUBPANELS, step, 0)
        ring_finish()
        for chunk in range(ROW_CHUNKS):
            row_pass(chunk)
        slabs_arrived()
        lax.fori_loop(0, SUBPANELS, lambda k, c: (update(k), c)[1], 0)

    @pl.when(no(is_root))
    def _():
        plan = {
            10: [(stage1, 0)], 16: [(stage2, 0)], 19: [(stage1, 1)], 22: [(stage3, 0)],
            26: [(stage2, 1), (stage4, 0)],
        }
        for chunk in range(ROW_CHUNKS):
            plan.setdefault(max(0, 3 * chunk - 3), []).append((row_first, chunk))
            plan.setdefault(5 + 3 * chunk, []).append((row_step, chunk))
            plan.setdefault(8 + 4 * chunk, []).append((row_pass, chunk))

        def one(n, _):
            ring_step(n)
            for when, actions in plan.items():
                @pl.when(n == when)
                def _():
                    for action, argument in actions:
                        action(argument)

            return 0

        lax.fori_loop(0, RING_STEPS, one, 0)
        stage3(1)
        ring_finish()
        stage1(2)
        stage2(2)
        stage5(0)
        stage4(1)
        stage3(2)
        pl.when(is_spreader)(
            lambda: (stage4(2), stage1(3), stage2(3), stage3(3), stage4(3)) and None
        )
        slabs_arrived()

        def some(k, _):
            update(k)
            for fixed in range(SUBPANELS - 1):
                @pl.when(k == fixed)
                def _():
                    if fixed == 0:
                        stage5(1)
                        pl.when(no(is_spreader))(lambda: (stage4(2), stage2(3)) and None)
                    if fixed == 1:
                        pl.when(no(is_spreader))(lambda: stage3(3))
                        stage5(2)
                    if fixed == 2:
                        pl.when(no(is_spreader))(lambda: stage4(3))
                        stage5(3)

            return 0

        lax.fori_loop(0, SUBPANELS, some, 0)

    top, left = row < SUBPANELS, col < SUBPANELS

    @pl.when(left)
    def _():
        o_ref[:, 0:NB] = column[...]

    @pl.when(top)
    def _():
        o_ref[0:NB, NB:] = jnp.zeros((NB, size - NB), F32)

    @pl.when(both(top, col > row))
    def _():
        o_ref[0:NB, 0:NB] = jnp.zeros((NB, NB), F32)

    @pl.when(both(top, col == row))
    def _():
        o_ref[0:NB, 0:NB] = jnp.where(iota_r >= iota_c, o_ref[0:NB, 0:NB], 0.0)

    pl.when(owner)(corner_copy(0, 0).wait_send)

    for k in range(SUBPANELS):
        group_sent(k)


def body(a):
    size = a.shape[0]
    dma = pltpu.SemaphoreType.DMA
    vmem = pltpu.VMEM
    return pl.pallas_call(
        factor_kernel,
        out_shape=jax.ShapeDtypeStruct(a.shape, F32),
        in_specs=[pl.BlockSpec(memory_space=pl.ANY)],
        out_specs=pl.BlockSpec(memory_space=pltpu.VMEM),
        scratch_shapes=[
            vmem((SUBPANELS, size, NB), F32),
            vmem((SUBPANELS, NB, size), F32),
            vmem((SUBPANELS, SUBPANELS, NB, NB), F32),
            vmem((SUBPANELS, SUBPANELS, NB, NB), F32),
            vmem((NB, 2 * NB), F32),
            vmem((2, size, NB), BF16),
            vmem((2, NB, size), BF16),
            vmem((size, NB), F32),
            dma((4,)),
            dma((1,)), dma((16,)),
            dma((ROW_CHUNKS, 2)), dma((ROW_CHUNKS, 2)),
            dma((ROW_CHUNKS, 5)), dma((ROW_CHUNKS, 2)), dma((ROW_CHUNKS, 2)),
            dma((2, 2, RING_CHUNKS)), dma((RING_CHUNKS,)), dma((2, 2, RING_CHUNKS)),
            dma((2,)), dma((2,)),
            dma((4,)), dma((4,)),
            dma((4, 15)), dma((4,)),
            dma((4, 7)), dma((4,)),
            dma((4, 3)), dma((4, 3)),
            dma((4, 3)), dma((4, 3)),
            dma((4,)), dma((4,)),
        ],
        compiler_params=pltpu.CompilerParams(
            collective_id=0, has_side_effects=True, vmem_limit_bytes=56 << 20
        ),
        name="factor_corner_and_update",
    )(a)


def solution(mesh):
    return jax.shard_map(
        body,
        mesh=mesh,
        in_specs=(P("row", "col"),),
        out_specs=P("row", "col"),
        check_vma=False,
    )
```

```python
import functools

import jax
import jax.numpy as jnp
from jax import lax
from jax.experimental import pallas as pl
from jax.experimental.pallas import tpu as pltpu
from jax.sharding import PartitionSpec as P

NB = 256
SUBPANELS = 4
MESH = pl.DeviceIdType.MESH
F32 = jnp.float32
BF16 = jnp.bfloat16


def split3(x):
    high = x.astype(BF16)
    rest = x - high.astype(F32)
    middle = rest.astype(BF16)
    low = (rest - middle.astype(F32)).astype(BF16)
    return high, middle, low


def split2(x):
    high = x.astype(BF16)
    return high, (x - high.astype(F32)).astype(BF16)


def dot_nn(a, b):
    return lax.dot_general(a, b, (((1,), (0,)), ((), ())), preferred_element_type=F32)


def dot_nt(a, b):
    return lax.dot_general(a, b, (((1,), (1,)), ((), ())), preferred_element_type=F32)


def dot3(dot, a, b):
    return dot(a[0], b[0]) + (dot(a[0], b[1]) + dot(a[1], b[0]))


def tree_sum(terms):
    while len(terms) > 1:
        terms = [sum(terms[i + 1 : i + 2], terms[i]) for i in range(0, len(terms), 2)]
    return terms[0]


def eliminate(tiles, s, first, active, iota):
    quarter, lane = divmod(first, 128)

    def spread(x):
        return jnp.broadcast_to(x, (8, 128))

    column = {
        t: [spread(tiles[t][quarter][:, lane + k : lane + k + 1]) for k in range(8)]
        for t in range(s, 4)
    }
    e = [[spread(column[s][k][i : i + 1, :]) if k <= i else None for k in range(8)] for i in range(8)]
    low = [[None] * 8 for _ in range(8)]
    inv = [[None] * 8 for _ in range(8)]
    for j in range(8):
        root = lax.rsqrt(e[j][j])
        for i in range(j + 1, 8):
            low[i][j] = e[i][j] * root
        for i in range(j + 1, 8):
            for k in range(j + 1, i + 1):
                e[i][k] = e[i][k] - low[i][j] * low[k][j]
        inv[j][j] = root
        for k in range(j):
            total = low[j][k] * inv[k][k]
            for m in range(k + 1, j):
                total = total + low[j][m] * inv[m][k]
            inv[j][k] = -(root * total)
    columns = []
    for k in range(8):
        value = inv[7][k]
        for i in range(6, k - 1, -1):
            value = jnp.where(iota == i, inv[i][k], value)
        if k > 0:
            value = jnp.where(iota < k, 0.0, value)
        columns.append(value)
    done = {
        q: tree_sum([columns[k] * spread(tiles[s][q][k : k + 1, :]) for k in range(8)])
        for q in active
    }
    for t in range(s + 1, 4):
        factor = [tree_sum([column[t][m] * inv[k][m] for m in range(k + 1)]) for k in range(8)]
        for q in active:
            tiles[t][q] = tiles[t][q] - tree_sum(
                [factor[k] * spread(done[q][k : k + 1, :]) for k in range(8)]
            )
    tiles[s].update(done)


def factor_block(work):
    iota = lax.broadcasted_iota(jnp.int32, (8, 128), 0)
    for slab in range(8):
        first = 32 * slab
        active = [0, 1, 2] if slab < 4 else [1, 2, 3]
        tiles = [
            {q: work[first + 8 * t : first + 8 * t + 8, 128 * q : 128 * q + 128] for q in active}
            for t in range(4)
        ]
        for s in range(4):
            eliminate(tiles, s, first + 8 * s, active, iota)
        for t in range(4):
            for q in active:
                work[first + 8 * t : first + 8 * t + 8, 128 * q : 128 * q + 128] = tiles[t][q]
        if slab == 7:
            break
        left = 128 * active[0]
        top = jnp.concatenate(
            [jnp.concatenate([tiles[t][q] for q in active], axis=1) for t in range(4)], axis=0
        )
        high, middle, low = split3(top)
        right = jnp.concatenate([high, middle, high, middle, low, high], axis=0)
        across = top[:, : 256 - left].T
        high, middle, low = split3(across)
        down = jnp.concatenate([high, high, middle, middle, high, low], axis=1)
        for begin, end in ((first + 32, first + 64), (first + 64, 256)):
            if begin < end:
                work[begin:end, left : left + 384] = work[begin:end, left : left + 384] - dot_nn(
                    down[begin - left : end - left], right
                )


ROW_CHUNKS = 6
RING_CHUNKS = 16
RING_LAG = 3
AHEAD = 2
RING_STEPS = max(RING_CHUNKS + 5 * RING_LAG, 9 + 4 * (ROW_CHUNKS - 1))


def factor_kernel(
    a_ref, o_ref,
    rows, cols, low, corner, work, p2, v2, column,
    local, c_send, c_recv, x_send, x_recv, y_send, y_recv, y_next, z_send, z_extra, z_recv,
    q_send, q_recv, r_send, r_recv, s_send, s_recv, t_send, t_recv,
    u_send, u_recv, w_send, w_recv, e_send, e_recv,
):
    size = a_ref.shape[0]
    row, col = lax.axis_index("row"), lax.axis_index("col")
    z, core = row // 2, row % 2
    x, y = col // 4, col % 4
    both, either, no = jnp.logical_and, jnp.logical_or, jnp.logical_not
    is_root = both(row == 0, col == 0)
    is_spreader = both(row == 1, col == 0)
    root, spreader = (0, 0), (1, 0)

    def at(zz, cc, xx, yy):
        return (zz * 2 + cc, xx * 4 + yy)

    def ring(step):
        return at((z + step) % 8, core, x, y)

    def plane(dx, dy):
        return at(z, core, (x + dx) % 4, (y + dy) % 4)

    pair = at(z, 1 - core, x, y)

    def remote(ref, send, recv, where, src=None):
        return pltpu.make_async_remote_copy(
            src_ref=ref if src is None else src, dst_ref=ref, send_sem=send, recv_sem=recv,
            device_id=where, device_id_type=MESH,
        )

    barrier = pltpu.get_barrier_semaphore()
    offsets = [(dx, dy) for dx in range(4) for dy in range(4) if dx or dy]
    peers = [ring(step) for step in range(1, 8)] + [plane(*o) for o in offsets] + [pair]
    for peer in peers:
        pl.semaphore_signal(barrier, inc=1, device_id=peer, device_id_type=MESH)
    owners = [(i, j) for i in range(SUBPANELS) for j in range(i + 1) if i or j]
    owner = both(both(row < SUBPANELS, col <= row), no(is_root))

    @pl.when(owner)
    def _():
        pl.semaphore_signal(barrier, inc=1, device_id=root, device_id_type=MESH)

    @pl.when(is_root)
    def _():
        for peer in owners:
            pl.semaphore_signal(barrier, inc=1, device_id=peer, device_id_type=MESH)

    keep = pltpu.make_async_copy(a_ref, o_ref, local.at[0])
    keep.start()
    own_cols = pltpu.make_async_copy(a_ref.at[0:NB, :], cols.at[row % SUBPANELS], local.at[1])
    own_rows = pltpu.make_async_copy(a_ref.at[:, 0:NB], rows.at[y], local.at[2])
    own_corner = pltpu.make_async_copy(a_ref.at[0:NB, 0:NB], corner.at[0, 0], local.at[3])
    pl.when(row < SUBPANELS)(own_cols.start)
    pl.when(x == 0)(own_rows.start)
    pl.when(is_root)(own_corner.start)
    total = len(peers) + jnp.where(owner, 1, 0) + jnp.where(is_root, len(owners), 0)
    pl.semaphore_wait(barrier, total)

    def corner_copy(i, j):
        return remote(
            corner.at[i, j], c_send.at[0], c_recv.at[i * SUBPANELS + j], root,
            src=a_ref.at[0:NB, 0:NB],
        )

    for i, j in owners:
        pl.when(both(row == i, col == j))(corner_copy(i, j).start)
    pl.when(row < SUBPANELS)(own_cols.wait)
    pl.when(x == 0)(own_rows.wait)

    def row_ref(source, chunk):
        length = size // ROW_CHUNKS
        return rows.at[source, chunk * length : (chunk + 1) * length, :]

    def row_half(source, chunk, part):
        length = size // ROW_CHUNKS // 2
        begin = (2 * chunk + part) * length
        return rows.at[source, begin : begin + length, :]

    def x_copy(chunk, side):
        return remote(
            row_ref(y, chunk), x_send.at[chunk, side], x_recv.at[chunk, 0], plane(1 + 2 * side, 0)
        )

    def x_half(chunk, side):
        return remote(
            row_half(y, chunk, side), x_send.at[chunk, 0], x_recv.at[chunk, side],
            plane(1 + 2 * side, 0),
        )

    beside_root = both(both(x == 0, z == 0), core == 0)
    direct = both(beside_root, y % 2 == 1)
    passing = no(both(beside_root, y % 2 == 0))

    def y_copy(chunk, side):
        return remote(
            row_ref(y, chunk), y_send.at[chunk, side], y_recv.at[chunk, side],
            plane(0, 1 + 2 * side),
        )

    def y_direct(chunk, source):
        return remote(
            row_ref(source, chunk), y_send.at[chunk, 4], y_next.at[chunk, 0], plane(0, 2)
        )

    def y_arrival(chunk, side):
        return remote(
            row_ref((y + 3 + 2 * side) % 4, chunk), y_send.at[chunk, side], y_recv.at[chunk, side],
            pair,
        )

    def y_half(chunk, side, source):
        return remote(
            row_half(source, chunk, side), y_send.at[chunk, 2 + side], y_next.at[chunk, side],
            plane(0, 1 + 2 * side),
        )

    def y_start(chunk):
        for side in range(2):
            y_copy(chunk, side).start()
        pl.when(direct)(y_direct(chunk, y).start)

    def row_first(chunk):
        pl.when(x == 0)(lambda: first_start(chunk))

    def row_step(chunk):
        for side in range(2):
            @pl.when(x == 1 + 2 * side)
            def _():
                x_copy(chunk, 0).wait_recv()
                x_half(chunk, side).start()

        @pl.when(x == 2)
        def _():
            for side in range(2):
                x_half(chunk, side).wait_recv()

        pl.when(x != 0)(lambda: y_start(chunk))

    def row_pass(chunk):
        for side in range(2):
            y_arrival(chunk, side).wait_recv()

            @pl.when(passing)
            def _():
                y_half(chunk, side, (y + 3 + 2 * side) % 4).start()

    def row_last(chunk):
        @pl.when(direct)
        def _():
            y_direct(chunk, (y + 2) % 4).wait_recv()

        @pl.when(no(direct))
        def _():
            for side in range(2):
                y_half(chunk, side, (y + 2) % 4).wait_recv()

    def rows_sent():
        for chunk in range(ROW_CHUNKS):
            for side in range(2):
                pl.when(x == 0)(x_copy(chunk, side).wait_send)
                pl.when(x == 1 + 2 * side)(x_half(chunk, side).wait_send)
                y_copy(chunk, side).wait_send()
                pl.when(passing)(y_half(chunk, side, y).wait_send)
            pl.when(direct)(y_direct(chunk, y).wait_send)

    def ring_ref(u, way, chunk):
        length = NB // 2 // RING_CHUNKS
        begin = pl.multiple_of(way * (NB // 2) + chunk * length, length)
        return cols.at[2 * u + core, pl.ds(begin, length), :]

    def distance(u, way):
        return (z - u + 8) % 8 if way == 0 else (u - z + 8) % 8

    def ring_copy(u, way, chunk):
        step = 1 if way == 0 else 7
        if (u, way) == (1, 1):
            where = at(jnp.where(z == 1, 7, (z + 7) % 8), core, x, y)
        else:
            where = ring(step)
        return remote(
            ring_ref(u, way, chunk), z_send.at[u, way, chunk], z_recv.at[u, way, chunk], where
        )

    def ring_second(chunk):
        return remote(ring_ref(1, 1, chunk), z_extra.at[chunk], z_recv.at[1, 1, chunk], ring(7))

    def ring_passes(u, way):
        passes = distance(u, way) < 7
        return both(passes, z != 0) if (u, way) == (1, 1) else passes

    def each_chunk(action):
        def one(chunk, _):
            action(chunk)
            return 0

        lax.fori_loop(0, RING_CHUNKS, one, 0)

    def slab_copy(u, which):
        return remote(cols.at[2 * u + which], q_send.at[u], q_recv.at[u], pair)

    def first_start(chunk):
        for side in range(2):
            x_copy(chunk, side).start()
        y_start(chunk)

    def ring_source(u, chunk, action):
        for way in range(2):
            action(ring_copy(u, way, chunk))
        if u == 1:
            action(ring_second(chunk))

    @pl.when(is_root)
    def _():
        for chunk in range(ROW_CHUNKS):
            first_start(chunk)
        each_chunk(lambda chunk: ring_source(0, chunk, lambda copy: copy.start()))

    def group(k, begin, length):
        return low.at[k, 0 : SUBPANELS - k, pl.ds(begin, length), :]

    def give(k):
        return remote(group(k, 0, NB), r_send.at[k], r_recv.at[k], spreader)

    def deal(k, dx, dy):
        piece = (4 * dy + dx) * 16
        return remote(
            group(k, piece, 16), s_send.at[k, 4 * dx + dy - 1], s_recv.at[k], (1, dx * 4 + dy)
        )

    mine = pl.multiple_of((4 * y + x) * 16, 16)

    def climb(k, step):
        return remote(group(k, mine, 16), t_send.at[k, step - 1], t_recv.at[k], ring(step))

    def spread_x(k, d):
        return remote(group(k, mine, 16), u_send.at[k, d - 1], u_recv.at[k, d - 1], plane(d, 0))

    def spread_x_arrival(k, d):
        begin = pl.multiple_of((4 * y + (x + 4 - d) % 4) * 16, 16)
        return remote(group(k, begin, 16), u_send.at[k, d - 1], u_recv.at[k, d - 1], pair)

    def spread_y(k, d):
        begin = pl.multiple_of(y * 64, 64)
        return remote(group(k, begin, 64), w_send.at[k, d - 1], w_recv.at[k, d - 1], plane(0, d))

    def spread_y_arrival(k, d):
        begin = pl.multiple_of((y + 4 - d) % 4 * 64, 64)
        return remote(group(k, begin, 64), w_send.at[k, d - 1], w_recv.at[k, d - 1], pair)

    def to_pair(k):
        return remote(group(k, 0, NB), e_send.at[k], e_recv.at[k], pair)

    def x_goes(d):
        return both(core == 1, no(both(both(z == 0, y == 0), (x + d) % 4 == 0)))

    def y_goes(d):
        return both(core == 1, no(both(both(z == 0, x == 0), (y + d) % 4 == 0)))

    takes = both(core == 1, no(is_spreader))

    def stage1(k):
        @pl.when(is_spreader)
        def _():
            give(k).wait_recv()
            for dx, dy in offsets:
                deal(k, dx, dy).start()

    def stage2(k):
        @pl.when(both(core == 1, z == 0))
        def _():
            @pl.when(no(is_spreader))
            def _():
                remote(group(k, mine, 16), r_send.at[k], s_recv.at[k], pair).wait_recv()

            for step in range(1, 8):
                climb(k, step).start()

    def stage3(k):
        @pl.when(both(core == 1, z != 0))
        def _():
            climb(k, 1).wait_recv()

        for d in range(1, 4):
            pl.when(x_goes(d))(spread_x(k, d).start)

    def stage4(k):
        @pl.when(takes)
        def _():
            for d in range(1, 4):
                spread_x_arrival(k, d).wait_recv()

        for d in range(1, 4):
            pl.when(y_goes(d))(spread_y(k, d).start)

    def stage5(k):
        @pl.when(takes)
        def _():
            for d in range(1, 4):
                spread_y_arrival(k, d).wait_recv()
            to_pair(k).start()

        @pl.when(both(core == 0, no(is_root)))
        def _():
            to_pair(k).wait_recv()

    def group_sent(k):
        pl.when(is_root)(give(k).wait_send)

        @pl.when(is_spreader)
        def _():
            for dx, dy in offsets:
                deal(k, dx, dy).wait_send()

        @pl.when(both(core == 1, z == 0))
        def _():
            for step in range(1, 8):
                climb(k, step).wait_send()

        for d in range(1, 4):
            pl.when(x_goes(d))(spread_x(k, d).wait_send)
            pl.when(y_goes(d))(spread_y(k, d).wait_send)
        pl.when(takes)(to_pair(k).wait_send)

    iota_r = lax.broadcasted_iota(jnp.int32, (NB, NB), 0)
    iota_c = lax.broadcasted_iota(jnp.int32, (NB, NB), 1)

    def ring_step(n):
        for u in range(2):
            @pl.when(both(z == u, n < RING_CHUNKS))
            def _():
                @pl.when(n >= AHEAD)
                def _():
                    ring_source(u, n - AHEAD, lambda copy: copy.wait_send())

                ring_source(u, n, lambda copy: copy.start())

        for u in range(2):
            for way in range(2):
                away = distance(u, way)
                chunk = n - RING_LAG * (away - 1)

                @pl.when(
                    both(both(away > 0, ring_passes(u, way)), both(chunk >= 0, chunk < RING_CHUNKS))
                )
                def _():
                    copy = ring_copy(u, way, chunk)
                    copy.wait_recv()
                    copy.start()

    def ring_finish():
        for u in range(2):
            for way in range(2):
                @pl.when(both(distance(u, way) > 0, no(ring_passes(u, way))))
                def _():
                    each_chunk(lambda chunk: ring_copy(u, way, chunk).wait_recv())

            slab_copy(u, core).start()

    def slabs_arrived():
        for chunk in range(ROW_CHUNKS):
            row_last(chunk)
        for u in range(2):
            slab_copy(u, 1 - core).wait_recv()
        keep.wait()
        rows_sent()
        for u in range(2):
            def left(chunk):
                @pl.when(both(z == u, either(is_root, chunk >= RING_CHUNKS - AHEAD)))
                def _():
                    ring_source(u, chunk, lambda copy: copy.wait_send())

                for way in range(2):
                    @pl.when(both(z != u, ring_passes(u, way)))
                    def _():
                        ring_copy(u, way, chunk).wait_send()

            each_chunk(left)
            slab_copy(u, core).wait_send()

    def left3(x, axis):
        high, rest = split2(x)
        return jnp.concatenate([high, high, rest], axis=axis)

    def right3(x, axis):
        high, rest = split2(x)
        return jnp.concatenate([high, rest, high], axis=axis)

    def update(k):
        p = dot_nt(left3(rows[k], 1), right3(low[k, 0], 1))
        p2[...] = left3(p, 1)
        v2[...] = right3(dot_nn(left3(low[k, 0], 1), right3(cols[k], 0)), 0)
        o_ref[...] = o_ref[...] - dot_nn(p2[...], v2[...])

        @pl.when(col == k)
        def _():
            column[...] = p

        def rest(m, _):
            block = low[k, m - k]
            rows[m] = rows[m] - dot_nt(p2[...], right3(block, 1))
            cols[m] = cols[m] - dot_nn(left3(block, 1), v2[...])
            return 0

        lax.fori_loop(k + 1, SUBPANELS, rest, 0)

    @pl.when(is_root)
    def _():
        own_corner.wait()
        eye = jnp.where(iota_r == iota_c, 1.0, 0.0).astype(F32)

        def step(k, _):
            work[:, 0:NB] = corner[k, k]
            work[:, NB : 2 * NB] = eye
            factor_block(work)
            inverse = jnp.where(iota_r >= iota_c, work[:, NB : 2 * NB], 0.0)
            low[k, 0] = inverse
            inv = split2(inverse)

            @pl.when(k == 0)
            def _():
                for i, j in owners:
                    corner_copy(i, j).wait_recv()

            def below(i, _):
                low[k, i - k] = dot3(dot_nt, split2(corner[i, k]), inv)
                return 0

            lax.fori_loop(k + 1, SUBPANELS, below, 0)
            for fixed in range(SUBPANELS):
                pl.when(k == fixed)(give(fixed).start)

            def trail(i, _):
                def inner(j, _):
                    corner[i, j] = corner[i, j] - dot3(
                        dot_nt, split2(low[k, i - k]), split2(low[k, j - k])
                    )
                    return 0

                return lax.fori_loop(k + 1, i + 1, inner, 0)

            return lax.fori_loop(k + 1, SUBPANELS, trail, 0)

        lax.fori_loop(0, SUBPANELS, step, 0)
        ring_finish()
        for chunk in range(ROW_CHUNKS):
            row_pass(chunk)
        slabs_arrived()
        lax.fori_loop(0, SUBPANELS, lambda k, c: (update(k), c)[1], 0)

    @pl.when(no(is_root))
    def _():
        plan = {
            10: [(stage1, 0)], 16: [(stage2, 0)], 19: [(stage1, 1)], 22: [(stage3, 0)],
            26: [(stage2, 1), (stage4, 0)],
        }
        for chunk in range(ROW_CHUNKS):
            plan.setdefault(max(0, 3 * chunk - 3), []).append((row_first, chunk))
            plan.setdefault(5 + 3 * chunk, []).append((row_step, chunk))
            plan.setdefault(8 + 4 * chunk, []).append((row_pass, chunk))

        def one(n, _):
            ring_step(n)
            for when, actions in plan.items():
                @pl.when(n == when)
                def _():
                    for action, argument in actions:
                        action(argument)

            return 0

        lax.fori_loop(0, RING_STEPS, one, 0)
        stage3(1)
        ring_finish()
        stage1(2)
        stage2(2)
        stage5(0)
        stage4(1)
        stage3(2)
        pl.when(is_spreader)(
            lambda: (stage4(2), stage1(3), stage2(3), stage3(3), stage4(3)) and None
        )
        slabs_arrived()

        def some(k, _):
            update(k)
            for fixed in range(SUBPANELS - 1):
                @pl.when(k == fixed)
                def _():
                    if fixed == 0:
                        stage5(1)
                        pl.when(no(is_spreader))(lambda: (stage4(2), stage2(3)) and None)
                    if fixed == 1:
                        pl.when(no(is_spreader))(lambda: stage3(3))
                        stage5(2)
                    if fixed == 2:
                        pl.when(no(is_spreader))(lambda: stage4(3))
                        stage5(3)

            return 0

        lax.fori_loop(0, SUBPANELS, some, 0)

    top, left = row < SUBPANELS, col < SUBPANELS

    @pl.when(left)
    def _():
        o_ref[:, 0:NB] = column[...]

    @pl.when(top)
    def _():
        o_ref[0:NB, NB:] = jnp.zeros((NB, size - NB), F32)

    @pl.when(both(top, col > row))
    def _():
        o_ref[0:NB, 0:NB] = jnp.zeros((NB, NB), F32)

    @pl.when(both(top, col == row))
    def _():
        o_ref[0:NB, 0:NB] = jnp.where(iota_r >= iota_c, o_ref[0:NB, 0:NB], 0.0)

    pl.when(owner)(corner_copy(0, 0).wait_send)

    for k in range(SUBPANELS):
        group_sent(k)


def body(a):
    size = a.shape[0]
    dma = pltpu.SemaphoreType.DMA
    vmem = pltpu.VMEM
    return pl.pallas_call(
        factor_kernel,
        out_shape=jax.ShapeDtypeStruct(a.shape, F32),
        in_specs=[pl.BlockSpec(memory_space=pl.ANY)],
        out_specs=pl.BlockSpec(memory_space=pltpu.VMEM),
        scratch_shapes=[
            vmem((SUBPANELS, size, NB), F32),
            vmem((SUBPANELS, NB, size), F32),
            vmem((SUBPANELS, SUBPANELS, NB, NB), F32),
            vmem((SUBPANELS, SUBPANELS, NB, NB), F32),
            vmem((NB, 2 * NB), F32),
            vmem((size, 3 * NB), BF16),
            vmem((3 * NB, size), BF16),
            vmem((size, NB), F32),
            dma((4,)),
            dma((1,)), dma((16,)),
            dma((ROW_CHUNKS, 2)), dma((ROW_CHUNKS, 2)),
            dma((ROW_CHUNKS, 5)), dma((ROW_CHUNKS, 2)), dma((ROW_CHUNKS, 2)),
            dma((2, 2, RING_CHUNKS)), dma((RING_CHUNKS,)), dma((2, 2, RING_CHUNKS)),
            dma((2,)), dma((2,)),
            dma((4,)), dma((4,)),
            dma((4, 15)), dma((4,)),
            dma((4, 7)), dma((4,)),
            dma((4, 3)), dma((4, 3)),
            dma((4, 3)), dma((4, 3)),
            dma((4,)), dma((4,)),
        ],
        compiler_params=pltpu.CompilerParams(
            collective_id=0, has_side_effects=True, vmem_limit_bytes=56 << 20
        ),
        name="factor_corner_and_update",
    )(a)


def solution(mesh):
    return jax.shard_map(
        body,
        mesh=mesh,
        in_specs=(P("row", "col"),),
        out_specs=P("row", "col"),
        check_vma=False,
    )
```

```python
import functools

import jax
import jax.numpy as jnp
from jax import lax
from jax.experimental import pallas as pl
from jax.experimental.pallas import tpu as pltpu
from jax.sharding import PartitionSpec as P

NB = 256
SUBPANELS = 4
MESH = pl.DeviceIdType.MESH
F32 = jnp.float32
BF16 = jnp.bfloat16


def split3(x):
    high = x.astype(BF16)
    rest = x - high.astype(F32)
    middle = rest.astype(BF16)
    low = (rest - middle.astype(F32)).astype(BF16)
    return high, middle, low


def split2(x):
    high = x.astype(BF16)
    return high, (x - high.astype(F32)).astype(BF16)


def dot_nn(a, b):
    return lax.dot_general(a, b, (((1,), (0,)), ((), ())), preferred_element_type=F32)


def dot_nt(a, b):
    return lax.dot_general(a, b, (((1,), (1,)), ((), ())), preferred_element_type=F32)


def dot3(dot, a, b):
    return dot(a[0], b[0]) + (dot(a[0], b[1]) + dot(a[1], b[0]))


def tree_sum(terms):
    while len(terms) > 1:
        terms = [sum(terms[i + 1 : i + 2], terms[i]) for i in range(0, len(terms), 2)]
    return terms[0]


def eliminate(tiles, s, first, active, iota):
    quarter, lane = divmod(first, 128)

    def spread(x):
        return jnp.broadcast_to(x, (8, 128))

    column = {
        t: [spread(tiles[t][quarter][:, lane + k : lane + k + 1]) for k in range(8)]
        for t in range(s, 4)
    }
    e = [[spread(column[s][k][i : i + 1, :]) if k <= i else None for k in range(8)] for i in range(8)]
    low = [[None] * 8 for _ in range(8)]
    inv = [[None] * 8 for _ in range(8)]
    for j in range(8):
        root = lax.rsqrt(e[j][j])
        for i in range(j + 1, 8):
            low[i][j] = e[i][j] * root
        for i in range(j + 1, 8):
            for k in range(j + 1, i + 1):
                e[i][k] = e[i][k] - low[i][j] * low[k][j]
        inv[j][j] = root
        for k in range(j):
            total = low[j][k] * inv[k][k]
            for m in range(k + 1, j):
                total = total + low[j][m] * inv[m][k]
            inv[j][k] = -(root * total)
    columns = []
    for k in range(8):
        value = inv[7][k]
        for i in range(6, k - 1, -1):
            value = jnp.where(iota == i, inv[i][k], value)
        if k > 0:
            value = jnp.where(iota < k, 0.0, value)
        columns.append(value)
    done = {
        q: tree_sum([columns[k] * spread(tiles[s][q][k : k + 1, :]) for k in range(8)])
        for q in active
    }
    for t in range(s + 1, 4):
        factor = [tree_sum([column[t][m] * inv[k][m] for m in range(k + 1)]) for k in range(8)]
        for q in active:
            tiles[t][q] = tiles[t][q] - tree_sum(
                [factor[k] * spread(done[q][k : k + 1, :]) for k in range(8)]
            )
    tiles[s].update(done)


def factor_block(work):
    iota = lax.broadcasted_iota(jnp.int32, (8, 128), 0)
    for slab in range(8):
        first = 32 * slab
        active = [0, 1, 2] if slab < 4 else [1, 2, 3]
        tiles = [
            {q: work[first + 8 * t : first + 8 * t + 8, 128 * q : 128 * q + 128] for q in active}
            for t in range(4)
        ]
        for s in range(4):
            eliminate(tiles, s, first + 8 * s, active, iota)
        for t in range(4):
            for q in active:
                work[first + 8 * t : first + 8 * t + 8, 128 * q : 128 * q + 128] = tiles[t][q]
        if slab == 7:
            break
        left = 128 * active[0]
        top = jnp.concatenate(
            [jnp.concatenate([tiles[t][q] for q in active], axis=1) for t in range(4)], axis=0
        )
        high, middle, low = split3(top)
        right = jnp.concatenate([high, middle, high, middle, low, high], axis=0)
        across = top[:, : 256 - left].T
        high, middle, low = split3(across)
        down = jnp.concatenate([high, high, middle, middle, high, low], axis=1)
        for begin, end in ((first + 32, first + 64), (first + 64, 256)):
            if begin < end:
                work[begin:end, left : left + 384] = work[begin:end, left : left + 384] - dot_nn(
                    down[begin - left : end - left], right
                )


ROW_CHUNKS = 6
RING_CHUNKS = 16
RING_LAG = 3
AHEAD = 2
RING_STEPS = max(RING_CHUNKS + 5 * RING_LAG, 9 + 4 * (ROW_CHUNKS - 1))


def factor_kernel(
    a_ref, o_ref,
    rows, cols, low, corner, work, p2, v2, column,
    local, c_send, c_recv, x_send, x_recv, y_send, y_recv, y_next, z_send, z_extra, z_recv,
    q_send, q_recv, r_send, r_recv, s_send, s_recv, t_send, t_recv,
    u_send, u_recv, w_send, w_recv, e_send, e_recv,
):
    size = a_ref.shape[0]
    row, col = lax.axis_index("row"), lax.axis_index("col")
    z, core = row // 2, row % 2
    x, y = col // 4, col % 4
    both, either, no = jnp.logical_and, jnp.logical_or, jnp.logical_not
    is_root = both(row == 0, col == 0)
    is_spreader = both(row == 1, col == 0)
    root, spreader = (0, 0), (1, 0)

    def at(zz, cc, xx, yy):
        return (zz * 2 + cc, xx * 4 + yy)

    def ring(step):
        return at((z + step) % 8, core, x, y)

    def plane(dx, dy):
        return at(z, core, (x + dx) % 4, (y + dy) % 4)

    pair = at(z, 1 - core, x, y)

    def remote(ref, send, recv, where, src=None):
        return pltpu.make_async_remote_copy(
            src_ref=ref if src is None else src, dst_ref=ref, send_sem=send, recv_sem=recv,
            device_id=where, device_id_type=MESH,
        )

    barrier = pltpu.get_barrier_semaphore()
    offsets = [(dx, dy) for dx in range(4) for dy in range(4) if dx or dy]
    peers = [ring(step) for step in range(1, 8)] + [plane(*o) for o in offsets] + [pair]
    for peer in peers:
        pl.semaphore_signal(barrier, inc=1, device_id=peer, device_id_type=MESH)
    owners = [(i, j) for i in range(SUBPANELS) for j in range(i + 1) if i or j]
    owner = both(both(row < SUBPANELS, col <= row), no(is_root))

    @pl.when(owner)
    def _():
        pl.semaphore_signal(barrier, inc=1, device_id=root, device_id_type=MESH)

    @pl.when(is_root)
    def _():
        for peer in owners:
            pl.semaphore_signal(barrier, inc=1, device_id=peer, device_id_type=MESH)

    keep = pltpu.make_async_copy(a_ref, o_ref, local.at[0])
    keep.start()
    own_cols = pltpu.make_async_copy(a_ref.at[0:NB, :], cols.at[row % SUBPANELS], local.at[1])
    own_rows = pltpu.make_async_copy(a_ref.at[:, 0:NB], rows.at[y], local.at[2])
    own_corner = pltpu.make_async_copy(a_ref.at[0:NB, 0:NB], corner.at[0, 0], local.at[3])
    pl.when(row < SUBPANELS)(own_cols.start)
    pl.when(x == 0)(own_rows.start)
    pl.when(is_root)(own_corner.start)
    total = len(peers) + jnp.where(owner, 1, 0) + jnp.where(is_root, len(owners), 0)
    pl.semaphore_wait(barrier, total)

    def corner_copy(i, j):
        return remote(
            corner.at[i, j], c_send.at[0], c_recv.at[i * SUBPANELS + j], root,
            src=a_ref.at[0:NB, 0:NB],
        )

    for i, j in owners:
        pl.when(both(row == i, col == j))(corner_copy(i, j).start)
    pl.when(row < SUBPANELS)(own_cols.wait)
    pl.when(x == 0)(own_rows.wait)

    def row_ref(source, chunk):
        length = size // ROW_CHUNKS
        return rows.at[source, chunk * length : (chunk + 1) * length, :]

    def row_half(source, chunk, part):
        length = size // ROW_CHUNKS // 2
        begin = (2 * chunk + part) * length
        return rows.at[source, begin : begin + length, :]

    def x_copy(chunk, side):
        return remote(
            row_ref(y, chunk), x_send.at[chunk, side], x_recv.at[chunk, 0], plane(1 + 2 * side, 0)
        )

    def x_half(chunk, side):
        return remote(
            row_half(y, chunk, side), x_send.at[chunk, 0], x_recv.at[chunk, side],
            plane(1 + 2 * side, 0),
        )

    beside_root = both(both(x == 0, z == 0), core == 0)
    direct = both(beside_root, y % 2 == 1)
    passing = no(both(beside_root, y % 2 == 0))

    def y_copy(chunk, side):
        return remote(
            row_ref(y, chunk), y_send.at[chunk, side], y_recv.at[chunk, side],
            plane(0, 1 + 2 * side),
        )

    def y_direct(chunk, source):
        return remote(
            row_ref(source, chunk), y_send.at[chunk, 4], y_next.at[chunk, 0], plane(0, 2)
        )

    def y_arrival(chunk, side):
        return remote(
            row_ref((y + 3 + 2 * side) % 4, chunk), y_send.at[chunk, side], y_recv.at[chunk, side],
            pair,
        )

    def y_half(chunk, side, source):
        return remote(
            row_half(source, chunk, side), y_send.at[chunk, 2 + side], y_next.at[chunk, side],
            plane(0, 1 + 2 * side),
        )

    def y_start(chunk):
        for side in range(2):
            y_copy(chunk, side).start()
        pl.when(direct)(y_direct(chunk, y).start)

    def row_first(chunk):
        pl.when(x == 0)(lambda: first_start(chunk))

    def row_step(chunk):
        for side in range(2):
            @pl.when(x == 1 + 2 * side)
            def _():
                x_copy(chunk, 0).wait_recv()
                x_half(chunk, side).start()

        @pl.when(x == 2)
        def _():
            for side in range(2):
                x_half(chunk, side).wait_recv()

        pl.when(x != 0)(lambda: y_start(chunk))

    def row_pass(chunk):
        for side in range(2):
            y_arrival(chunk, side).wait_recv()

            @pl.when(passing)
            def _():
                y_half(chunk, side, (y + 3 + 2 * side) % 4).start()

    def row_last(chunk):
        @pl.when(direct)
        def _():
            y_direct(chunk, (y + 2) % 4).wait_recv()

        @pl.when(no(direct))
        def _():
            for side in range(2):
                y_half(chunk, side, (y + 2) % 4).wait_recv()

    def rows_sent():
        for chunk in range(ROW_CHUNKS):
            for side in range(2):
                pl.when(x == 0)(x_copy(chunk, side).wait_send)
                pl.when(x == 1 + 2 * side)(x_half(chunk, side).wait_send)
                y_copy(chunk, side).wait_send()
                pl.when(passing)(y_half(chunk, side, y).wait_send)
            pl.when(direct)(y_direct(chunk, y).wait_send)

    def ring_ref(u, way, chunk):
        length = NB // 2 // RING_CHUNKS
        begin = pl.multiple_of(way * (NB // 2) + chunk * length, length)
        return cols.at[2 * u + core, pl.ds(begin, length), :]

    def distance(u, way):
        return (z - u + 8) % 8 if way == 0 else (u - z + 8) % 8

    def ring_copy(u, way, chunk):
        step = 1 if way == 0 else 7
        if (u, way) == (1, 1):
            where = at(jnp.where(z == 1, 7, (z + 7) % 8), core, x, y)
        else:
            where = ring(step)
        return remote(
            ring_ref(u, way, chunk), z_send.at[u, way, chunk], z_recv.at[u, way, chunk], where
        )

    def ring_second(chunk):
        return remote(ring_ref(1, 1, chunk), z_extra.at[chunk], z_recv.at[1, 1, chunk], ring(7))

    def ring_passes(u, way):
        passes = distance(u, way) < 7
        return both(passes, z != 0) if (u, way) == (1, 1) else passes

    def each_chunk(action):
        def one(chunk, _):
            action(chunk)
            return 0

        lax.fori_loop(0, RING_CHUNKS, one, 0)

    def slab_copy(u, which):
        return remote(cols.at[2 * u + which], q_send.at[u], q_recv.at[u], pair)

    def first_start(chunk):
        for side in range(2):
            x_copy(chunk, side).start()
        y_start(chunk)

    def ring_source(u, chunk, action):
        for way in range(2):
            action(ring_copy(u, way, chunk))
        if u == 1:
            action(ring_second(chunk))

    @pl.when(is_root)
    def _():
        for chunk in range(ROW_CHUNKS):
            first_start(chunk)
        each_chunk(lambda chunk: ring_source(0, chunk, lambda copy: copy.start()))

    def group(k, begin, length):
        return low.at[k, 0 : SUBPANELS - k, pl.ds(begin, length), :]

    def give(k):
        return remote(group(k, 0, NB), r_send.at[k], r_recv.at[k], spreader)

    def deal(k, dx, dy):
        piece = (4 * dy + dx) * 16
        return remote(
            group(k, piece, 16), s_send.at[k, 4 * dx + dy - 1], s_recv.at[k], (1, dx * 4 + dy)
        )

    mine = pl.multiple_of((4 * y + x) * 16, 16)

    def climb(k, step):
        return remote(group(k, mine, 16), t_send.at[k, step - 1], t_recv.at[k], ring(step))

    def spread_x(k, d):
        return remote(group(k, mine, 16), u_send.at[k, d - 1], u_recv.at[k, d - 1], plane(d, 0))

    def spread_x_arrival(k, d):
        begin = pl.multiple_of((4 * y + (x + 4 - d) % 4) * 16, 16)
        return remote(group(k, begin, 16), u_send.at[k, d - 1], u_recv.at[k, d - 1], pair)

    def spread_y(k, d):
        begin = pl.multiple_of(y * 64, 64)
        return remote(group(k, begin, 64), w_send.at[k, d - 1], w_recv.at[k, d - 1], plane(0, d))

    def spread_y_arrival(k, d):
        begin = pl.multiple_of((y + 4 - d) % 4 * 64, 64)
        return remote(group(k, begin, 64), w_send.at[k, d - 1], w_recv.at[k, d - 1], pair)

    def to_pair(k):
        return remote(group(k, 0, NB), e_send.at[k], e_recv.at[k], pair)

    def x_goes(d):
        return both(core == 1, no(both(both(z == 0, y == 0), (x + d) % 4 == 0)))

    def y_goes(d):
        return both(core == 1, no(both(both(z == 0, x == 0), (y + d) % 4 == 0)))

    takes = both(core == 1, no(is_spreader))

    def stage1(k):
        @pl.when(is_spreader)
        def _():
            give(k).wait_recv()
            for dx, dy in offsets:
                deal(k, dx, dy).start()

    def stage2(k):
        @pl.when(both(core == 1, z == 0))
        def _():
            @pl.when(no(is_spreader))
            def _():
                remote(group(k, mine, 16), r_send.at[k], s_recv.at[k], pair).wait_recv()

            for step in range(1, 8):
                climb(k, step).start()

    def stage3(k):
        @pl.when(both(core == 1, z != 0))
        def _():
            climb(k, 1).wait_recv()

        for d in range(1, 4):
            pl.when(x_goes(d))(spread_x(k, d).start)

    def stage4(k):
        @pl.when(takes)
        def _():
            for d in range(1, 4):
                spread_x_arrival(k, d).wait_recv()

        for d in range(1, 4):
            pl.when(y_goes(d))(spread_y(k, d).start)

    def stage5(k):
        @pl.when(takes)
        def _():
            for d in range(1, 4):
                spread_y_arrival(k, d).wait_recv()
            to_pair(k).start()

        @pl.when(both(core == 0, no(is_root)))
        def _():
            to_pair(k).wait_recv()

    def group_sent(k):
        pl.when(is_root)(give(k).wait_send)

        @pl.when(is_spreader)
        def _():
            for dx, dy in offsets:
                deal(k, dx, dy).wait_send()

        @pl.when(both(core == 1, z == 0))
        def _():
            for step in range(1, 8):
                climb(k, step).wait_send()

        for d in range(1, 4):
            pl.when(x_goes(d))(spread_x(k, d).wait_send)
            pl.when(y_goes(d))(spread_y(k, d).wait_send)
        pl.when(takes)(to_pair(k).wait_send)

    iota_r = lax.broadcasted_iota(jnp.int32, (NB, NB), 0)
    iota_c = lax.broadcasted_iota(jnp.int32, (NB, NB), 1)

    def ring_step(n):
        for u in range(2):
            @pl.when(both(z == u, n < RING_CHUNKS))
            def _():
                @pl.when(n >= AHEAD)
                def _():
                    ring_source(u, n - AHEAD, lambda copy: copy.wait_send())

                ring_source(u, n, lambda copy: copy.start())

        for u in range(2):
            for way in range(2):
                away = distance(u, way)
                chunk = n - RING_LAG * (away - 1)

                @pl.when(
                    both(both(away > 0, ring_passes(u, way)), both(chunk >= 0, chunk < RING_CHUNKS))
                )
                def _():
                    copy = ring_copy(u, way, chunk)
                    copy.wait_recv()
                    copy.start()

    def ring_finish():
        for u in range(2):
            for way in range(2):
                @pl.when(both(distance(u, way) > 0, no(ring_passes(u, way))))
                def _():
                    each_chunk(lambda chunk: ring_copy(u, way, chunk).wait_recv())

            slab_copy(u, core).start()

    def slabs_arrived():
        for chunk in range(ROW_CHUNKS):
            row_last(chunk)
        for u in range(2):
            slab_copy(u, 1 - core).wait_recv()
        keep.wait()
        rows_sent()
        for u in range(2):
            def left(chunk):
                @pl.when(both(z == u, either(is_root, chunk >= RING_CHUNKS - AHEAD)))
                def _():
                    ring_source(u, chunk, lambda copy: copy.wait_send())

                for way in range(2):
                    @pl.when(both(z != u, ring_passes(u, way)))
                    def _():
                        ring_copy(u, way, chunk).wait_send()

            each_chunk(left)
            slab_copy(u, core).wait_send()

    def left3(x, axis):
        high, rest = split2(x)
        return jnp.concatenate([high, high, rest], axis=axis)

    def right3(x, axis):
        high, rest = split2(x)
        return jnp.concatenate([high, rest, high], axis=axis)

    def update(k):
        p = dot_nt(left3(rows[k], 1), right3(low[k, 0], 1))
        p2[...] = left3(p, 1)
        v2[...] = right3(dot_nn(left3(low[k, 0], 1), right3(cols[k], 0)), 0)
        o_ref[...] = o_ref[...] - dot_nn(p2[...], v2[...])

        @pl.when(col == k)
        def _():
            column[...] = p

        def rest(m, _):
            block = low[k, m - k]
            rows[m] = rows[m] - dot_nt(p2[...], right3(block, 1))
            cols[m] = cols[m] - dot_nn(left3(block, 1), v2[...])
            return 0

        lax.fori_loop(k + 1, SUBPANELS, rest, 0)

    @pl.when(is_root)
    def _():
        own_corner.wait()
        eye = jnp.where(iota_r == iota_c, 1.0, 0.0).astype(F32)

        def step(k, _):
            work[:, 0:NB] = corner[k, k]
            work[:, NB : 2 * NB] = eye
            factor_block(work)
            inverse = jnp.where(iota_r >= iota_c, work[:, NB : 2 * NB], 0.0)
            low[k, 0] = inverse
            inv = right3(inverse, 1)

            @pl.when(k == 0)
            def _():
                for i, j in owners:
                    corner_copy(i, j).wait_recv()

            def below(i, _):
                low[k, i - k] = dot_nt(left3(corner[i, k], 1), inv)
                return 0

            lax.fori_loop(k + 1, SUBPANELS, below, 0)
            for fixed in range(SUBPANELS):
                pl.when(k == fixed)(give(fixed).start)

            def trail(i, _):
                def inner(j, _):
                    corner[i, j] = corner[i, j] - dot_nt(
                        left3(low[k, i - k], 1), right3(low[k, j - k], 1)
                    )
                    return 0

                return lax.fori_loop(k + 1, i + 1, inner, 0)

            return lax.fori_loop(k + 1, SUBPANELS, trail, 0)

        lax.fori_loop(0, SUBPANELS, step, 0)
        ring_finish()
        for chunk in range(ROW_CHUNKS):
            row_pass(chunk)
        slabs_arrived()
        lax.fori_loop(0, SUBPANELS, lambda k, c: (update(k), c)[1], 0)

    @pl.when(no(is_root))
    def _():
        plan = {
            10: [(stage1, 0)], 16: [(stage2, 0)], 19: [(stage1, 1)], 22: [(stage3, 0)],
            26: [(stage2, 1), (stage4, 0)],
        }
        for chunk in range(ROW_CHUNKS):
            plan.setdefault(max(0, 3 * chunk - 3), []).append((row_first, chunk))
            plan.setdefault(5 + 3 * chunk, []).append((row_step, chunk))
            plan.setdefault(8 + 4 * chunk, []).append((row_pass, chunk))

        def one(n, _):
            ring_step(n)
            for when, actions in plan.items():
                @pl.when(n == when)
                def _():
                    for action, argument in actions:
                        action(argument)

            return 0

        lax.fori_loop(0, RING_STEPS, one, 0)
        stage3(1)
        ring_finish()
        stage1(2)
        stage2(2)
        stage5(0)
        stage4(1)
        stage3(2)
        pl.when(is_spreader)(
            lambda: (stage4(2), stage1(3), stage2(3), stage3(3), stage4(3)) and None
        )
        slabs_arrived()

        def some(k, _):
            update(k)
            for fixed in range(SUBPANELS - 1):
                @pl.when(k == fixed)
                def _():
                    if fixed == 0:
                        stage5(1)
                        pl.when(no(is_spreader))(lambda: (stage4(2), stage2(3)) and None)
                    if fixed == 1:
                        pl.when(no(is_spreader))(lambda: stage3(3))
                        stage5(2)
                    if fixed == 2:
                        pl.when(no(is_spreader))(lambda: stage4(3))
                        stage5(3)

            return 0

        lax.fori_loop(0, SUBPANELS, some, 0)

    top, left = row < SUBPANELS, col < SUBPANELS

    @pl.when(left)
    def _():
        o_ref[:, 0:NB] = column[...]

    @pl.when(top)
    def _():
        o_ref[0:NB, NB:] = jnp.zeros((NB, size - NB), F32)

    @pl.when(both(top, col > row))
    def _():
        o_ref[0:NB, 0:NB] = jnp.zeros((NB, NB), F32)

    @pl.when(both(top, col == row))
    def _():
        o_ref[0:NB, 0:NB] = jnp.where(iota_r >= iota_c, o_ref[0:NB, 0:NB], 0.0)

    pl.when(owner)(corner_copy(0, 0).wait_send)

    for k in range(SUBPANELS):
        group_sent(k)


def body(a):
    size = a.shape[0]
    dma = pltpu.SemaphoreType.DMA
    vmem = pltpu.VMEM
    return pl.pallas_call(
        factor_kernel,
        out_shape=jax.ShapeDtypeStruct(a.shape, F32),
        in_specs=[pl.BlockSpec(memory_space=pl.ANY)],
        out_specs=pl.BlockSpec(memory_space=pltpu.VMEM),
        scratch_shapes=[
            vmem((SUBPANELS, size, NB), F32),
            vmem((SUBPANELS, NB, size), F32),
            vmem((SUBPANELS, SUBPANELS, NB, NB), F32),
            vmem((SUBPANELS, SUBPANELS, NB, NB), F32),
            vmem((NB, 2 * NB), F32),
            vmem((size, 3 * NB), BF16),
            vmem((3 * NB, size), BF16),
            vmem((size, NB), F32),
            dma((4,)),
            dma((1,)), dma((16,)),
            dma((ROW_CHUNKS, 2)), dma((ROW_CHUNKS, 2)),
            dma((ROW_CHUNKS, 5)), dma((ROW_CHUNKS, 2)), dma((ROW_CHUNKS, 2)),
            dma((2, 2, RING_CHUNKS)), dma((RING_CHUNKS,)), dma((2, 2, RING_CHUNKS)),
            dma((2,)), dma((2,)),
            dma((4,)), dma((4,)),
            dma((4, 15)), dma((4,)),
            dma((4, 7)), dma((4,)),
            dma((4, 3)), dma((4, 3)),
            dma((4, 3)), dma((4, 3)),
            dma((4,)), dma((4,)),
        ],
        compiler_params=pltpu.CompilerParams(
            collective_id=0, has_side_effects=True, vmem_limit_bytes=56 << 20
        ),
        name="factor_corner_and_update",
    )(a)


def solution(mesh):
    return jax.shard_map(
        body,
        mesh=mesh,
        in_specs=(P("row", "col"),),
        out_specs=P("row", "col"),
        check_vma=False,
    )
```
